256 devices in a mesh: gx: 16 (over x, y_lo, core), gy: 16 (over z, y_hi).
Axes of the slice: x: 4, y: 4 (y_hi: 2, y_lo: 2; y = y_hi * 2 + y_lo), z: 8, core: 2. Of those that a mesh axis runs over, the one named last changes fastest.
Arguments:
- positions: float32 [3, 16, 16, 16384], P(None, 'gx', 'gy'), may hold values from 0 to 2
- velocities: float32 [3, 16, 16, 16384], P(None, 'gx', 'gy'), may hold values from -6 to 6
- charges: float32 [16, 16, 16384], P('gx', 'gy'), may hold values from -1 to 1
- repel_root: float32 [16, 16, 16384], P('gx', 'gy'), may hold values from 0.001 to 0.01
- disperse_root: float32 [16, 16, 16384], P('gx', 'gy'), may hold values from 0.02 to 0.2
- inverse_mass: float32 [16, 16, 16384], P('gx', 'gy'), may hold values from 0.06 to 1
- move: int32 [16, 16, 128], P('gx', 'gy'), may hold values from 0 to 8, as said below
- tiles: int32 [16, 16, 2304, 2], P('gx', 'gy'), may hold values from 0 to 575
Outputs:
- new_positions: float32 [3, 16, 16, 18432], P(None, 'gx', 'gy')
- new_velocities: float32 [3, 16, 16, 18432], P(None, 'gx', 'gy')
- forces: float32 [3, 16, 16, 18432], P(None, 'gx', 'gy')
The draws below stay inside these ranges and needn't reach their ends.
Inputs may be any that keep to these rules, and one draw needn't show every extreme that they name: `move`: on every owner at most 2 blocks carry any one code from 1 to 8, so an owner receives at most 144 blocks; in every draw some owner sends exactly 2 blocks toward a neighbour and some owner receives exactly 144.
All inputs are finite; a program needn't handle non-finite values.
Results may differ from the reference program's by a relative error of at most 0.0003.
Values sent between devices are 32-bit elements; how exact they have to be, the bound alone decides.
No kernel may reach another device: no remote copies, remote signals or barrier semaphores. Data moves between devices by JAX's collectives and lax.ppermute only.
A program may use at most 128 MiB of HBM per device.

```python
import math
import jax
import jax.numpy as jnp
from jax import lax

BLOCK = 128
ILEN = 8
TILES = 2
NB = 128
HOME = 16384
ICL = 2304
ZONE_BLOCKS = 576
CELLS_X = 16
CELLS_Y = 16


def draw_move(key, part):
    key = jax.random.fold_in(key, 11)
    quota = max(1, NB // 64)
    key_sink, key_counts, key_perm = jax.random.split(key, 3)
    sink_x = jax.random.randint(key_sink, (), 0, CELLS_X)
    sink_y = jax.random.randint(jax.random.fold_in(key_sink, 1), (), 0, CELLS_Y)
    counts = jax.random.randint(key_counts, (CELLS_X, CELLS_Y, 8), 0, quota + 1)
    grid_x = jnp.arange(CELLS_X, dtype=jnp.int32)[:, None, None]
    grid_y = jnp.arange(CELLS_Y, dtype=jnp.int32)[None, :, None]
    step_x = jnp.array([1, -1, 0, 0, 1, 1, -1, -1], dtype=jnp.int32)
    step_y = jnp.array([0, 0, 1, -1, 1, -1, 1, -1], dtype=jnp.int32)
    aimed = ((grid_x + step_x) % CELLS_X == sink_x) & ((grid_y + step_y) % CELLS_Y == sink_y)
    counts = jnp.where(aimed, quota, counts)
    at_sink = (grid_x == sink_x) & (grid_y == sink_y)
    counts = jnp.where(at_sink, 0, counts)
    ends = jnp.cumsum(counts, axis=-1)
    blocks = jnp.arange(NB, dtype=jnp.int32)[None, None, :]
    codes = jnp.sum((blocks[..., None] >= ends[:, :, None, :]).astype(jnp.int32), axis=-1) + 1
    codes = jnp.where(blocks < ends[..., -1:], codes, 0)
    keys = jax.random.split(key_perm, CELLS_X * CELLS_Y)
    orders = jax.vmap(lambda sub_key: jax.random.permutation(sub_key, NB))(keys).reshape(CELLS_X, CELLS_Y, NB)
    return jnp.take_along_axis(codes, orders, axis=-1).astype(jnp.int32)


def plant(values, rng, least, top_value):
    extent = values.shape
    spot = [jax.random.randint(jax.random.fold_in(rng, axis), (), 0, extent[axis]) for axis in range(len(extent))]
    values = values.at[tuple(spot)].set(least)
    longest = extent.index(max(extent))
    spot[longest] = (spot[longest] + 1) % extent[longest]
    return values.at[tuple(spot)].set(top_value)


def level_of(key, extent, cuts, smallest, top_value):
    def one(position, blocks):
        heights = jax.random.uniform(jax.random.fold_in(jax.random.fold_in(key, 6), position), (blocks,), jnp.float32, smallest / len(cuts), top_value / len(cuts))
        return jnp.repeat(jnp.exp(heights), extent[position] // blocks).reshape((-1,) + (1,) * (len(extent) - position - 1))

    loudness = one(*cuts[0])
    for cut in cuts[1:]:
        loudness = loudness * one(*cut)
    return loudness


def gaussian(key, extent, deviation, reach, cuts=(), held_as=jnp.bfloat16):
    gain = level_of(key, extent, cuts, -0.22, 0.18) if cuts else 1.0
    drawn = jax.random.normal(key, extent, jnp.float32) * deviation * gain
    return jnp.minimum(jnp.maximum(drawn, -reach), reach).astype(held_as)


def setup_inputs(seed: int = 0) -> dict:
    seeds = jax.random.split(jax.random.key(seed), 9)
    positions = jnp.clip(2.0 * jax.random.uniform(seeds[0], (3, CELLS_X, CELLS_Y, HOME), jnp.float32) ** level_of(seeds[0], (3, CELLS_X, CELLS_Y, HOME), ((1, 16), (2, 16)), -0.2, 0.2), 0.0, 2.0)
    velocities = gaussian(seeds[1], (3, CELLS_X, CELLS_Y, HOME), 1.0, 6.0, ((1, 16), (2, 16)), jnp.float32)
    charges = jnp.clip(jax.random.uniform(seeds[2], (CELLS_X, CELLS_Y, HOME), jnp.float32, -1.0, 1.0) * level_of(seeds[2], (CELLS_X, CELLS_Y, HOME), ((0, 16), (1, 16)), -0.4, 0.0), -1.0, 1.0)
    repel_root = jnp.clip(jnp.exp(math.log(0.01) - 2.30258502 * jax.random.uniform(seeds[3], (CELLS_X, CELLS_Y, HOME), jnp.float32) ** level_of(seeds[3], (CELLS_X, CELLS_Y, HOME), ((0, 16), (1, 16)), -0.2, 0.2)), 0.001, 0.01)
    disperse_root = jnp.clip(jnp.exp(math.log(0.2) - 2.3025851 * jax.random.uniform(seeds[4], (CELLS_X, CELLS_Y, HOME), jnp.float32) ** level_of(seeds[4], (CELLS_X, CELLS_Y, HOME), ((0, 16), (1, 16)), -0.2, 0.2)), 0.02, 0.2)
    inverse_mass = jnp.clip(jnp.exp(math.log(1.0) - 2.8134107 * jax.random.uniform(seeds[5], (CELLS_X, CELLS_Y, HOME), jnp.float32) ** level_of(seeds[5], (CELLS_X, CELLS_Y, HOME), ((0, 16), (1, 16)), -0.2, 0.2)), 0.06, 1.0)
    move = draw_move(jax.random.fold_in(seeds[8], 71), 0)
    tiles = plant(jax.random.randint(seeds[7], (CELLS_X, CELLS_Y, ICL, TILES), 0, ZONE_BLOCKS), jax.random.fold_in(seeds[7], 1), 0, ZONE_BLOCKS - 1).astype(jnp.int32)
    return {"positions": positions, "velocities": velocities, "charges": charges, "repel_root": repel_root, "disperse_root": disperse_root, "inverse_mass": inverse_mass, "move": move, "tiles": tiles}


CELL = 2.0
TSTEP = 0.05
BETA = 2.0
FLOOR_SQ = 0.25
EWALD_COEF = 2.0 * BETA / 1.7724538509055159
OFFSETS = ((0, 0), (1, 0), (-1, 0), (0, 1), (0, -1), (1, 1), (1, -1), (-1, 1), (-1, -1))

def compact(blocks, chosen, width):
    nblk = chosen.shape[-1]
    ranks = jnp.cumsum(chosen.astype(jnp.int32), axis=-1, dtype=jnp.int32) - 1
    slots = jnp.arange(width, dtype=jnp.int32)
    onehot = chosen[..., None, :] & (ranks[..., None, :] == slots[:, None])
    source = lax.optimization_barrier(jnp.sum(onehot.astype(jnp.int32) * jnp.arange(nblk, dtype=jnp.int32), axis=-1, dtype=jnp.int32))
    filled = jnp.any(onehot, axis=-1)
    picked = jnp.take_along_axis(blocks, source[None, ..., None], axis=-2)
    picked = jnp.where(filled[None, ..., None], picked, jnp.float32(0.0))
    count = lax.optimization_barrier(jnp.sum(chosen.astype(jnp.int32), axis=-1, dtype=jnp.int32))
    return (picked, count)

def arrange(pool, counts, nblk, quota, capacity):
    starts = jnp.cumsum(counts, axis=0, dtype=jnp.int32) - counts
    total = lax.optimization_barrier(jnp.sum(counts, axis=0, dtype=jnp.int32))
    slots = jnp.arange(capacity, dtype=jnp.int32)
    group = lax.optimization_barrier(jnp.sum((starts[1:, ..., None] <= slots).astype(jnp.int32), axis=0, dtype=jnp.int32))
    base = jnp.where(group == 0, 0, nblk + (group - 1) * quota).astype(jnp.int32)
    codes = jnp.arange(9, dtype=jnp.int32).reshape((9,) + (1,) * counts.ndim)
    begin = lax.optimization_barrier(jnp.sum(jnp.where(group[None] == codes, starts[..., None], 0), axis=0, dtype=jnp.int32))
    valid = slots < total[..., None]
    index = jnp.where(valid, base + slots - begin, 0).astype(jnp.int32)
    picked = jnp.take_along_axis(pool, index[None, ..., None], axis=-2)
    return jnp.where(valid[None, ..., None], picked, jnp.float32(0.0))

def tile_forces(home, zones, tiles):
    capacity = home.shape[1]
    clusters = capacity * BLOCK // ILEN
    width = 128
    rounds = clusters // width
    atoms_i = home.reshape(6, rounds, width, ILEN).transpose(1, 0, 2, 3)
    tile_ids = tiles.reshape(rounds, width, tiles.shape[-1])
    cluster_ids = jnp.arange(clusters, dtype=jnp.int32).reshape(rounds, width)
    inner = jnp.arange(ILEN, dtype=jnp.int32)
    outer = jnp.arange(BLOCK, dtype=jnp.int32)

    def one_round(operands):
        left, listed, cluster = operands
        right = zones[:, listed]
        delta = left[:3, :, None, :, None] - right[:3, :, :, None, :]
        dist_sq = lax.optimization_barrier(jnp.sum(delta * delta, axis=0))
        floored = jnp.maximum(dist_sq, FLOOR_SQ)
        inverse = 1.0 / floored
        radius = jnp.sqrt(floored)
        qprod = left[3][:, None, :, None] * right[3][:, :, None, :]
        coul = qprod * (jax.scipy.special.erfc(BETA * radius) / radius + EWALD_COEF * jnp.exp(-BETA * BETA * floored)) * inverse
        repel = left[4][:, None, :, None] * right[4][:, :, None, :]
        disperse = left[5][:, None, :, None] * right[5][:, :, None, :]
        cube = inverse * inverse * inverse
        ljterm = (12.0 * repel * cube * cube - 6.0 * disperse * cube) * inverse
        switch = jnp.maximum(1.0 - dist_sq, 0.0)
        same_block = listed == cluster[:, None] // 16
        mol_i = (cluster[:, None] % 16 * ILEN + inner) // 4
        mol_j = outer // 4
        excluded = same_block[:, :, None, None] & (mol_i[:, None, :, None] == mol_j)
        scalar = jnp.where(excluded, jnp.float32(0.0), (coul + ljterm) * switch * switch)
        vectors = scalar[None] * delta
        on_i = lax.optimization_barrier(jnp.sum(vectors, axis=(2, 4)))
        on_j = -lax.optimization_barrier(jnp.sum(vectors, axis=3))
        return (on_i, on_j)
    on_i, on_j = lax.map(one_round, (atoms_i, tile_ids, cluster_ids))
    on_home = on_i.transpose(1, 0, 2, 3).reshape(3, capacity, BLOCK)
    flat_j = on_j.transpose(0, 2, 3, 1, 4).reshape(-1, 3, BLOCK)
    on_zones = jax.ops.segment_sum(flat_j, tiles.reshape(-1), num_segments=4 * capacity)
    return (on_home, on_zones.transpose(1, 0, 2))

def reference(positions, velocities, charges, repel_root, disperse_root, inverse_mass, move, tiles):
    cells_x, cells_y = (positions.shape[1], positions.shape[2])
    nblk = move.shape[-1]
    quota = max(1, nblk // 64)
    capacity = nblk + 8 * quota
    table = jnp.concatenate([positions, velocities, charges[None], repel_root[None], disperse_root[None], inverse_mass[None]], axis=0)
    table = table.reshape(10, cells_x, cells_y, nblk, BLOCK)
    pieces = []
    tallies = []
    for code in range(9):
        step_x, step_y = OFFSETS[code]
        moved = table.at[0].add(-step_x * CELL).at[1].add(-step_y * CELL)
        picked, count = compact(moved, move == code, nblk if code == 0 else quota)
        pieces.append(jnp.roll(picked, (step_x, step_y), axis=(1, 2)))
        tallies.append(jnp.roll(count, (step_x, step_y), axis=(0, 1)))
    pool = jnp.concatenate(pieces, axis=3)
    counts = jnp.stack(tallies)
    home = arrange(pool, counts, nblk, quota, capacity)
    coords = jnp.concatenate([home[0:3], home[6:9]], axis=0)

    def device_forces(index):
        place_x = index // cells_y
        place_y = index % cells_y

        def fetch(at_x, at_y):
            return coords[:, at_x % cells_x, at_y % cells_y]
        own = fetch(place_x, place_y)
        east = fetch(place_x + 1, place_y).at[0].add(CELL)
        north = fetch(place_x, place_y + 1).at[1].add(CELL)
        corner = fetch(place_x + 1, place_y + 1).at[0].add(CELL).at[1].add(CELL)
        zones = jnp.concatenate([own, east, north, corner], axis=1)
        return tile_forces(own, zones, tiles[place_x, place_y])
    on_home, on_zones = lax.map(device_forces, jnp.arange(cells_x * cells_y, dtype=jnp.int32))
    on_home = on_home.reshape(cells_x, cells_y, 3, capacity, BLOCK).transpose(2, 0, 1, 3, 4)
    zoned = on_zones.reshape(cells_x, cells_y, 3, 4, capacity, BLOCK).transpose(2, 3, 0, 1, 4, 5)
    total = on_home + zoned[:, 0]
    total = total + jnp.roll(zoned[:, 1], 1, axis=1)
    total = total + jnp.roll(zoned[:, 2], 1, axis=2)
    total = total + jnp.roll(zoned[:, 3], (1, 1), axis=(1, 2))
    new_velocities = home[3:6] + TSTEP * home[9][None] * total
    new_positions = home[0:3] + TSTEP * new_velocities
    shape_out = (3, cells_x, cells_y, capacity * BLOCK)
    return (new_positions.reshape(shape_out), new_velocities.reshape(shape_out), total.reshape(shape_out))
```

```python
import functools

import jax
import jax.numpy as jnp
from jax import lax
from jax.experimental import pallas as pl
from jax.experimental.pallas import tpu as pltpu
from jax.sharding import PartitionSpec as P

BLOCK = 128
NB = 128
CAPACITY = 144
CELL = 2.0
TSTEP = 0.05
OFFSETS = ((0, 0), (1, 0), (-1, 0), (0, 1), (0, -1), (1, 1), (1, -1), (-1, 1), (-1, -1))
RECIP_GAP = (
    0.004694723058491945,
    5.942236423492432,
    -13.92039680480957,
    18.602458953857422,
    -16.470346450805664,
    9.659473419189453,
    -3.41253399848938,
    0.5484030246734619,
)


def passed_along(value, step_x, step_y):
    nx, ny = lax.axis_size("gx"), lax.axis_size("gy")
    if step_y == 0:
        return lax.ppermute(value, "gx", [(s, (s + step_x) % nx) for s in range(nx)])
    if step_x == 0:
        return lax.ppermute(value, "gy", [(s, (s + step_y) % ny) for s in range(ny)])
    pairs = [
        (i * ny + j, ((i + step_x) % nx) * ny + (j + step_y) % ny)
        for i in range(nx)
        for j in range(ny)
    ]
    return lax.ppermute(value, ("gx", "gy"), pairs)


def pack_kernel(move, pos, vel, chg, rep, dis, inv, stay, parcels, staying, tally):
    zero = jnp.zeros((8, BLOCK), jnp.float32)
    for f in range(10):
        for u in range(CAPACITY // 8):
            stay[f, 8 * u : 8 * u + 8, :] = zero
    for p in range(9):
        for u in range(3):
            parcels[p, 8 * u : 8 * u + 8, :] = zero
        tally[p] = 0

    def rows(k):
        at = pl.ds(k, 1)
        return [pos[d, at, :] for d in range(3)] + [vel[d, at, :] for d in range(3)] + [
            ref[at, :] for ref in (chg, rep, dis, inv)
        ]

    def one(k, kept):
        code = move[k]
        values = rows(k)
        for f in range(10):
            stay[f, pl.ds(kept, 1), :] = values[f]
        seen = tally[code]
        tally[code] = seen + 1
        slot = jnp.where(code == 0, 0, jnp.minimum(seen, 1)) * 10
        for f in range(10):
            parcels[code, pl.ds(slot + f, 1), :] = values[f]
        return kept + jnp.where(code == 0, 1, 0)

    kept = lax.fori_loop(0, NB, one, 0)
    for f in range(10):
        stay[f, pl.ds(kept, 1), :] = zero[0:1]
    staying[0] = kept
    for code in range(1, 9):
        step_x, step_y = OFFSETS[code]
        for n in range(2):
            if step_x != 0:
                parcels[code, 10 * n : 10 * n + 1, :] = parcels[code, 10 * n : 10 * n + 1, :] - step_x * CELL
            if step_y != 0:
                parcels[code, 10 * n + 1 : 10 * n + 2, :] = parcels[code, 10 * n + 1 : 10 * n + 2, :] - step_y * CELL
        parcels[code, 20:21, :] = jnp.broadcast_to(tally[code], (1, BLOCK)).astype(jnp.float32)


def arrive_kernel(staying, stay, *refs):
    parcels, coords, rest, held = refs[:8], refs[8], refs[9], refs[10]
    for f in range(10):
        held[f, 0:CAPACITY, :] = stay[f]
    counts = jnp.concatenate([p[20:21, :] for p in parcels], axis=0).astype(jnp.int32)
    at = staying[0]
    for code in range(8):
        count = counts[code, 0]
        for n in range(2):
            for f in range(10):
                held[f, pl.ds(at, 1), :] = parcels[code][10 * n + f : 10 * n + f + 1, :]
            at = at + jnp.where(count > n, 1, 0)
    for f in range(10):
        held[f, pl.ds(at, 1), :] = jnp.zeros((1, BLOCK), jnp.float32)
    for k, f in enumerate((0, 1, 2, 6, 7, 8)):
        coords[k] = held[f, 0:CAPACITY, :]
    for k, f in enumerate((3, 4, 5, 9)):
        rest[k] = held[f, 0:CAPACITY, :]


def update_kernel(home, east, north, corner, coords, rest, new_x, new_v, total):
    for d in range(3):
        force = home[d] + east[d] + north[d] + corner[d]
        fresh = rest[d] + TSTEP * rest[3] * force
        total[d] = force
        new_v[d] = fresh
        new_x[d] = coords[d] + TSTEP * fresh


def listed(b):
    return (b // 8) * 256 + (b % 8) * 16


def pair_kernel(tiles, home, east, north, corner, fh, fe, fn, fc, zone, ac0, ac1, ac2, ibuf0, ibuf1, vbuf0, vbuf1, wbuf, *, T=2, mxu=True):
    acc=(ac0,ac1,ac2)
    sub = lax.broadcasted_iota(jnp.int32,(8,128),0)
    lane = lax.broadcasted_iota(jnp.int32,(8,128),1)
    rel = lane//4 - sub//4
    for c in range(16):
        wbuf[c]=jnp.where(rel==2*c,0.0,1.0)
    wbuf[16]=jnp.ones((8,128),jnp.float32)
    for z,(ref,sx,sy) in enumerate(((home,0.,0.),(east,2.,0.),(north,0.,2.),(corner,2.,2.))):
        for f in range(6):
            v = ref[f]
            if f==0 and sx: v=v+sx
            if f==1 and sy: v=v+sy
            zone[f, pl.ds(z*CAPACITY,CAPACITY), :] = v
    zero = jnp.zeros((8,128),jnp.float32)
    def clear(k,_):
        for u in range(16):
            for d in range(3):
                acc[d][pl.ds(pl.multiple_of(k*128,128)+8*u,8),:]=zero
        return 0
    lax.fori_loop(0,(4*CAPACITY)//16,clear,0)

    def row(f,j):
        return jnp.broadcast_to(zone[f, pl.ds(j,1), :],(8,128))
    SC=jnp.where(sub==4,12.0,jnp.where(sub==5,6.0,1.0)).astype(jnp.float32)
    kk=lax.broadcasted_iota(jnp.int32,(24,768),0); nn=lax.broadcasted_iota(jnp.int32,(24,768),1)
    pick=jnp.where(kk%8==nn//128,1.0,0.0).astype(jnp.bfloat16)

    def spread(b,ibuf):
        feat = jnp.concatenate([home[f, pl.ds(b,1), :] for f in range(6)]+[jnp.zeros((2,128),jnp.float32)],axis=0)*SC
        hi=feat.astype(jnp.bfloat16).astype(jnp.float32); r=feat-hi
        mid=r.astype(jnp.bfloat16).astype(jnp.float32); lo=r-mid
        ft=jnp.concatenate([hi,mid,lo],axis=0).T.astype(jnp.bfloat16)
        out=jnp.dot(ft,pick,preferred_element_type=jnp.float32)
        for f in range(6):
            for c in range(16): ibuf[f,c]=out[8*c:8*c+8,128*f:128*f+128]

    def settle(b,vbuf):
        tots=[]
        for c in range(16):
            tot=None
            for t in range(T):
                j8=pl.multiple_of(tiles[listed(b) + (128 * t + c)]*8,8)
                v=[vbuf[d,t,c] for d in range(3)]
                for d in range(3):
                    acc[d][pl.ds(j8,8),:]=acc[d][pl.ds(j8,8),:]+v[d]
                tot=v if tot is None else [p+q for p,q in zip(tot,v)]
            tots.append(tot)
        cc=[]
        for c in range(16):
            r=[jnp.sum(tots[c][d],axis=1,keepdims=True) for d in range(3)]
            cc.append(jnp.where(lane==0,r[0],jnp.where(lane==1,r[1],r[2])))
        m=jnp.concatenate(cc,axis=0)[:, :8].T
        for d in range(3):
            fh[d,pl.ds(b,1),:]=m[d:d+1]

    def block(b,ibuf,vbuf):
        for c in range(16):
            xi,yi,zi,qi,ai,bi=[ibuf[f,c] for f in range(6)]
            for t in range(T):
                j=tiles[listed(b) + (128 * t + c)]
                dx=xi-row(0,j); dy=yi-row(1,j); dz=zi-row(2,j)
                r2=dx*dx+dy*dy+dz*dz
                w=jnp.maximum(wbuf[jnp.where(j==b,c,16)]-r2,0.0)
                s=jnp.clip(r2,0.25,1.0)
                rs=lax.rsqrt(s)
                inv=rs*rs
                cube=inv*inv*inv
                h=RECIP_GAP[-1]
                for n in range(len(RECIP_GAP)-2,-1,-1):
                    h=h*s+RECIP_GAP[n]
                g=(qi*row(3,j))*(rs-h)+cube*((ai*row(4,j))*cube-bi*row(5,j))
                g=g*(inv*(w*w))
                vbuf[0,t,c]=g*dx
                vbuf[1,t,c]=g*dy
                vbuf[2,t,c]=g*dz

    spread(0,ibuf0)
    for d in range(3):
        for t in range(T):
            for c in range(16): vbuf1[d,t,c]=zero
    def two(k,_):
        b=2*k
        settle(jnp.maximum(b-1,0),vbuf1)
        spread(b+1,ibuf1)
        block(b,ibuf0,vbuf0)
        settle(b,vbuf0)
        spread(jnp.minimum(b+2,CAPACITY-1),ibuf0)
        block(b+1,ibuf1,vbuf1)
        return 0
    lax.fori_loop(0,CAPACITY//2,two,0)
    settle(CAPACITY-1,vbuf1)
    for d in range(3):
        for z,ref in enumerate((fh,fe,fn,fc)):
            def red(k,_):
                for u in range(3):
                    k8=pl.multiple_of(k*24+8*u,8)
                    r=[acc[d][pl.ds((z*CAPACITY+k8)*8+q,8,stride=8),:] for q in range(8)]
                    r=((r[0]+r[1])+(r[2]+r[3]))+((r[4]+r[5])+(r[6]+r[7]))
                    if z==0: ref[d,pl.ds(k8,8),:]=ref[d,pl.ds(k8,8),:]-r
                    else: ref[d,pl.ds(k8,8),:]=-r
                return 0
            lax.fori_loop(0,CAPACITY//24,red,0)


VM = pl.BlockSpec(memory_space=pltpu.VMEM)
SM = pl.BlockSpec(memory_space=pltpu.SMEM)
PARAMS = pltpu.CompilerParams(vmem_limit_bytes=48 * 1024 * 1024)


def planes(count, rows=CAPACITY):
    return jax.ShapeDtypeStruct((count, rows, BLOCK), jnp.float32)


def body(positions, velocities, charges, repel_root, disperse_root, inverse_mass, move, tiles):
    stay, parcels, staying = pl.pallas_call(
        pack_kernel,
        out_shape=(planes(10), planes(9, 24), jax.ShapeDtypeStruct((1,), jnp.int32)),
        in_specs=[SM] + [VM] * 6,
        out_specs=(VM, VM, SM),
        scratch_shapes=[pltpu.SMEM((9,), jnp.int32)],
        compiler_params=PARAMS,
        name="pack",
    )(
        move.reshape(NB),
        positions.reshape(3, NB, BLOCK),
        velocities.reshape(3, NB, BLOCK),
        charges.reshape(NB, BLOCK),
        repel_root.reshape(NB, BLOCK),
        disperse_root.reshape(NB, BLOCK),
        inverse_mass.reshape(NB, BLOCK),
    )
    arrived = [passed_along(parcels[code], *OFFSETS[code]) for code in range(1, 9)]
    coords, rest = pl.pallas_call(
        arrive_kernel,
        out_shape=(planes(6), planes(4)),
        in_specs=[SM] + [VM] * 9,
        out_specs=(VM, VM),
        scratch_shapes=[pltpu.VMEM((10, CAPACITY + 8, BLOCK), jnp.float32)],
        compiler_params=PARAMS,
        name="arrive",
    )(staying, stay, *arrived)
    east = passed_along(coords, -1, 0)
    north = passed_along(coords, 0, -1)
    corner = passed_along(coords, -1, -1)
    on_home, on_east, on_north, on_corner = pl.pallas_call(
        pair_kernel,
        out_shape=(planes(3),) * 4,
        in_specs=[SM] + [VM] * 4,
        out_specs=(VM,) * 4,
        scratch_shapes=[pltpu.VMEM((6,4 * CAPACITY,128),jnp.float32)]+[pltpu.VMEM((4 * CAPACITY*8,128),jnp.float32)]*3+[pltpu.VMEM((6,16,8,128),jnp.float32)]*2+[pltpu.VMEM((3,2,16,8,128),jnp.float32)]*2+[pltpu.VMEM((17,8,128),jnp.float32)],
        compiler_params=PARAMS,
        name="pair",
    )(tiles.reshape(18, 128, 2).transpose(0, 2, 1).reshape(-1), coords, east, north, corner)
    from_east = passed_along(on_east, 1, 0)
    from_north = passed_along(on_north, 0, 1)
    from_corner = passed_along(on_corner, 1, 1)
    out = pl.pallas_call(
        update_kernel,
        out_shape=(planes(3),) * 3,
        in_specs=[VM] * 6,
        out_specs=(VM,) * 3,
        compiler_params=PARAMS,
        name="update",
    )(on_home, from_east, from_north, from_corner, coords, rest)
    return tuple(value.reshape(3, 1, 1, CAPACITY * BLOCK) for value in out)


def solution(mesh):
    vector = P(None, "gx", "gy", None)
    scalar = P("gx", "gy", None)
    return jax.shard_map(
        body,
        mesh=mesh,
        in_specs=(vector, vector) + (scalar,) * 5 + (P("gx", "gy", None, None),),
        out_specs=(vector,) * 3,
        check_vma=False,
    )
```

```python
import functools

import jax
import jax.numpy as jnp
from jax import lax
from jax.experimental import pallas as pl
from jax.experimental.pallas import tpu as pltpu
from jax.sharding import PartitionSpec as P

BLOCK = 128
NB = 128
CAPACITY = 144
CELL = 2.0
TSTEP = 0.05
OFFSETS = ((0, 0), (1, 0), (-1, 0), (0, 1), (0, -1), (1, 1), (1, -1), (-1, 1), (-1, -1))
RECIP_GAP = (
    0.004694723058491945,
    5.942236423492432,
    -13.92039680480957,
    18.602458953857422,
    -16.470346450805664,
    9.659473419189453,
    -3.41253399848938,
    0.5484030246734619,
)


def passed_along(value, step_x, step_y):
    nx, ny = lax.axis_size("gx"), lax.axis_size("gy")
    if step_y == 0:
        return lax.ppermute(value, "gx", [(s, (s + step_x) % nx) for s in range(nx)])
    if step_x == 0:
        return lax.ppermute(value, "gy", [(s, (s + step_y) % ny) for s in range(ny)])
    pairs = [
        (i * ny + j, ((i + step_x) % nx) * ny + (j + step_y) % ny)
        for i in range(nx)
        for j in range(ny)
    ]
    return lax.ppermute(value, ("gx", "gy"), pairs)


def pack_kernel(*refs):
    sources, (stay, parcels, staying), scratch = refs[:7], refs[7:10], refs[10:]
    move, pos, vel, chg, rep, dis, inv = scratch[:7]
    tally, arrival = scratch[7:]
    copies = [
        pltpu.make_async_copy(source, held, arrival.at[k])
        for k, (source, held) in enumerate(zip(sources, scratch))
    ]
    for copy in copies:
        copy.start()
    zero = jnp.zeros((8, BLOCK), jnp.float32)
    for f in range(10):
        for u in range(CAPACITY // 8):
            stay[f, 8 * u : 8 * u + 8, :] = zero
    for p in range(9):
        for u in range(3):
            parcels[p, 8 * u : 8 * u + 8, :] = zero
        tally[p] = 0
    for copy in copies:
        copy.wait()

    def rows(k):
        at = pl.ds(k, 1)
        return [pos[d, at, :] for d in range(3)] + [vel[d, at, :] for d in range(3)] + [
            ref[at, :] for ref in (chg, rep, dis, inv)
        ]

    def one(k, kept):
        code = move[k]
        values = rows(k)
        for f in range(10):
            stay[f, pl.ds(kept, 1), :] = values[f]
        seen = tally[code]
        tally[code] = seen + 1
        slot = jnp.where(code == 0, 0, jnp.minimum(seen, 1)) * 10
        for f in range(10):
            parcels[code, pl.ds(slot + f, 1), :] = values[f]
        return kept + jnp.where(code == 0, 1, 0)

    kept = lax.fori_loop(0, NB, one, 0)
    for f in range(10):
        stay[f, pl.ds(kept, 1), :] = zero[0:1]
    staying[0] = kept
    for code in range(1, 9):
        step_x, step_y = OFFSETS[code]
        for n in range(2):
            if step_x != 0:
                parcels[code, 10 * n : 10 * n + 1, :] = parcels[code, 10 * n : 10 * n + 1, :] - step_x * CELL
            if step_y != 0:
                parcels[code, 10 * n + 1 : 10 * n + 2, :] = parcels[code, 10 * n + 1 : 10 * n + 2, :] - step_y * CELL
        parcels[code, 20:21, :] = jnp.broadcast_to(tally[code], (1, BLOCK)).astype(jnp.float32)


def arrive_kernel(staying, stay, *refs):
    parcels, coords, rest, held = refs[:8], refs[8], refs[9], refs[10]
    for f in range(10):
        held[f, 0:CAPACITY, :] = stay[f]
    counts = jnp.concatenate([p[20:21, :] for p in parcels], axis=0).astype(jnp.int32)
    at = staying[0]
    for code in range(8):
        count = counts[code, 0]
        for n in range(2):
            for f in range(10):
                held[f, pl.ds(at, 1), :] = parcels[code][10 * n + f : 10 * n + f + 1, :]
            at = at + jnp.where(count > n, 1, 0)
    for f in range(10):
        held[f, pl.ds(at, 1), :] = jnp.zeros((1, BLOCK), jnp.float32)
    for k, f in enumerate((0, 1, 2, 6, 7, 8)):
        coords[k] = held[f, 0:CAPACITY, :]
    for k, f in enumerate((3, 4, 5, 9)):
        rest[k] = held[f, 0:CAPACITY, :]


def update_kernel(home, east, north, coords, rest, new_x, new_v, total):
    for d in range(3):
        force = home[d] + east[d] + north[d]
        fresh = rest[d] + TSTEP * rest[3] * force
        total[d] = force
        new_v[d] = fresh
        new_x[d] = coords[d] + TSTEP * fresh


def listed(b):
    return (b // 8) * 256 + (b % 8) * 16


def pair_kernel(tiles, home, east, north, corner, fh, fx, fn, zone, ac0, ac1, ac2, ibuf0, ibuf1, vbuf0, vbuf1, wbuf, *, T=2, mxu=True):
    acc=(ac0,ac1,ac2)
    sub = lax.broadcasted_iota(jnp.int32,(8,128),0)
    lane = lax.broadcasted_iota(jnp.int32,(8,128),1)
    rel = lane//4 - sub//4
    for c in range(16):
        wbuf[c]=jnp.where(rel==2*c,0.0,1.0)
    wbuf[16]=jnp.ones((8,128),jnp.float32)
    for z,(ref,sx,sy) in enumerate(((home,0.,0.),(east,2.,0.),(north,0.,2.),(corner,2.,2.))):
        for f in range(6):
            v = ref[f]
            if f==0 and sx: v=v+sx
            if f==1 and sy: v=v+sy
            zone[f, pl.ds(z*CAPACITY,CAPACITY), :] = v
    zero = jnp.zeros((8,128),jnp.float32)
    def clear(k,_):
        for u in range(16):
            for d in range(3):
                acc[d][pl.ds(pl.multiple_of(k*128,128)+8*u,8),:]=zero
        return 0
    lax.fori_loop(0,(4*CAPACITY)//16,clear,0)

    def row(f,j):
        return jnp.broadcast_to(zone[f, pl.ds(j,1), :],(8,128))
    SC=jnp.where(sub==4,12.0,jnp.where(sub==5,6.0,1.0)).astype(jnp.float32)
    kk=lax.broadcasted_iota(jnp.int32,(24,768),0); nn=lax.broadcasted_iota(jnp.int32,(24,768),1)
    pick=jnp.where(kk%8==nn//128,1.0,0.0).astype(jnp.bfloat16)

    def spread(b,ibuf):
        feat = jnp.concatenate([home[f, pl.ds(b,1), :] for f in range(6)]+[jnp.zeros((2,128),jnp.float32)],axis=0)*SC
        hi=feat.astype(jnp.bfloat16).astype(jnp.float32); r=feat-hi
        mid=r.astype(jnp.bfloat16).astype(jnp.float32); lo=r-mid
        ft=jnp.concatenate([hi,mid,lo],axis=0).T.astype(jnp.bfloat16)
        out=jnp.dot(ft,pick,preferred_element_type=jnp.float32)
        for f in range(6):
            for c in range(16): ibuf[f,c]=out[8*c:8*c+8,128*f:128*f+128]

    def settle(b,vbuf):
        tots=[]
        for c in range(16):
            tot=None
            for t in range(T):
                j8=pl.multiple_of(tiles[listed(b) + (128 * t + c)]*8,8)
                v=[vbuf[d,t,c] for d in range(3)]
                for d in range(3):
                    acc[d][pl.ds(j8,8),:]=acc[d][pl.ds(j8,8),:]+v[d]
                tot=v if tot is None else [p+q for p,q in zip(tot,v)]
            tots.append(tot)
        cc=[]
        for c in range(16):
            r=[jnp.sum(tots[c][d],axis=1,keepdims=True) for d in range(3)]
            cc.append(jnp.where(lane==0,r[0],jnp.where(lane==1,r[1],r[2])))
        m=jnp.concatenate(cc,axis=0)[:, :8].T
        for d in range(3):
            fh[d,pl.ds(b,1),:]=m[d:d+1]

    def block(b,ibuf,vbuf):
        for c in range(16):
            xi,yi,zi,qi,ai,bi=[ibuf[f,c] for f in range(6)]
            for t in range(T):
                j=tiles[listed(b) + (128 * t + c)]
                dx=xi-row(0,j); dy=yi-row(1,j); dz=zi-row(2,j)
                r2=dx*dx+dy*dy+dz*dz
                w=jnp.maximum(wbuf[jnp.where(j==b,c,16)]-r2,0.0)
                s=jnp.clip(r2,0.25,1.0)
                rs=lax.rsqrt(s)
                inv=rs*rs
                cube=inv*inv*inv
                h=RECIP_GAP[-1]
                for n in range(len(RECIP_GAP)-2,-1,-1):
                    h=h*s+RECIP_GAP[n]
                g=(qi*row(3,j))*(rs-h)+cube*((ai*row(4,j))*cube-bi*row(5,j))
                g=g*(inv*(w*w))
                vbuf[0,t,c]=g*dx
                vbuf[1,t,c]=g*dy
                vbuf[2,t,c]=g*dz

    spread(0,ibuf0)
    for d in range(3):
        for t in range(T):
            for c in range(16): vbuf1[d,t,c]=zero
    def two(k,_):
        b=2*k
        settle(jnp.maximum(b-1,0),vbuf1)
        spread(b+1,ibuf1)
        block(b,ibuf0,vbuf0)
        settle(b,vbuf0)
        spread(jnp.minimum(b+2,CAPACITY-1),ibuf0)
        block(b+1,ibuf1,vbuf1)
        return 0
    lax.fori_loop(0,CAPACITY//2,two,0)
    settle(CAPACITY-1,vbuf1)
    for d in range(3):
        for z,(ref,o) in enumerate(((fh,0),(fx,0),(fn,0),(fx,3))):
            def red(k,_):
                for u in range(3):
                    k8=pl.multiple_of(k*24+8*u,8)
                    r=[acc[d][pl.ds((z*CAPACITY+k8)*8+q,8,stride=8),:] for q in range(8)]
                    r=((r[0]+r[1])+(r[2]+r[3]))+((r[4]+r[5])+(r[6]+r[7]))
                    if z==0: ref[o+d,pl.ds(k8,8),:]=ref[o+d,pl.ds(k8,8),:]-r
                    else: ref[o+d,pl.ds(k8,8),:]=-r
                return 0
            lax.fori_loop(0,CAPACITY//24,red,0)


VM = pl.BlockSpec(memory_space=pltpu.VMEM)
SM = pl.BlockSpec(memory_space=pltpu.SMEM)
PARAMS = pltpu.CompilerParams(vmem_limit_bytes=48 * 1024 * 1024)


def planes(count, rows=CAPACITY):
    return jax.ShapeDtypeStruct((count, rows, BLOCK), jnp.float32)


def body(positions, velocities, charges, repel_root, disperse_root, inverse_mass, move, tiles):
    stay, parcels, staying = pl.pallas_call(
        pack_kernel,
        out_shape=(planes(10), planes(9, 24), jax.ShapeDtypeStruct((1,), jnp.int32)),
        in_specs=[pl.BlockSpec(memory_space=pltpu.HBM)] * 7,
        out_specs=(VM, VM, SM),
        scratch_shapes=[pltpu.SMEM((NB,), jnp.int32)]
        + [pltpu.VMEM((3, NB, BLOCK), jnp.float32)] * 2
        + [pltpu.VMEM((NB, BLOCK), jnp.float32)] * 4
        + [pltpu.SMEM((9,), jnp.int32), pltpu.SemaphoreType.DMA((7,))],
        compiler_params=PARAMS,
        name="pack",
    )(
        move.reshape(NB),
        positions.reshape(3, NB, BLOCK),
        velocities.reshape(3, NB, BLOCK),
        charges.reshape(NB, BLOCK),
        repel_root.reshape(NB, BLOCK),
        disperse_root.reshape(NB, BLOCK),
        inverse_mass.reshape(NB, BLOCK),
    )
    arrived = [passed_along(parcels[code], *OFFSETS[code]) for code in range(1, 9)]
    coords, rest = pl.pallas_call(
        arrive_kernel,
        out_shape=(planes(6), planes(4)),
        in_specs=[SM] + [VM] * 9,
        out_specs=(VM, VM),
        scratch_shapes=[pltpu.VMEM((10, CAPACITY + 8, BLOCK), jnp.float32)],
        compiler_params=PARAMS,
        name="arrive",
    )(staying, stay, *arrived)
    east = passed_along(coords, -1, 0)
    north = passed_along(coords, 0, -1)
    corner = passed_along(north, -1, 0)
    on_home, on_x, on_north = pl.pallas_call(
        pair_kernel,
        out_shape=(planes(3), planes(6), planes(3)),
        in_specs=[SM] + [VM] * 4,
        out_specs=(VM,) * 3,
        scratch_shapes=[pltpu.VMEM((6,4 * CAPACITY,128),jnp.float32)]+[pltpu.VMEM((4 * CAPACITY*8,128),jnp.float32)]*3+[pltpu.VMEM((6,16,8,128),jnp.float32)]*2+[pltpu.VMEM((3,2,16,8,128),jnp.float32)]*2+[pltpu.VMEM((17,8,128),jnp.float32)],
        compiler_params=PARAMS,
        name="pair",
    )(tiles.reshape(18, 128, 2).transpose(0, 2, 1).reshape(-1), coords, east, north, corner)
    from_x = passed_along(on_x, 1, 0)
    from_north = passed_along(on_north + from_x[3:6], 0, 1)
    out = pl.pallas_call(
        update_kernel,
        out_shape=(planes(3),) * 3,
        in_specs=[VM] * 5,
        out_specs=(VM,) * 3,
        compiler_params=PARAMS,
        name="update",
    )(on_home, from_x, from_north, coords, rest)
    return tuple(value.reshape(3, 1, 1, CAPACITY * BLOCK) for value in out)


def solution(mesh):
    vector = P(None, "gx", "gy", None)
    scalar = P("gx", "gy", None)
    return jax.shard_map(
        body,
        mesh=mesh,
        in_specs=(vector, vector) + (scalar,) * 5 + (P("gx", "gy", None, None),),
        out_specs=(vector,) * 3,
        check_vma=False,
    )
```

```python
import functools

import jax
import jax.numpy as jnp
from jax import lax
from jax.experimental import pallas as pl
from jax.experimental.pallas import tpu as pltpu
from jax.sharding import PartitionSpec as P

BLOCK = 128
NB = 128
CAPACITY = 144
CELL = 2.0
TSTEP = 0.05
OFFSETS = ((0, 0), (1, 0), (-1, 0), (0, 1), (0, -1), (1, 1), (1, -1), (-1, 1), (-1, -1))
RECIP_GAP = (
    0.004694723058491945,
    5.942236423492432,
    -13.92039680480957,
    18.602458953857422,
    -16.470346450805664,
    9.659473419189453,
    -3.41253399848938,
    0.5484030246734619,
)


def passed_along(value, step_x, step_y):
    nx, ny = lax.axis_size("gx"), lax.axis_size("gy")
    if step_y == 0:
        return lax.ppermute(value, "gx", [(s, (s + step_x) % nx) for s in range(nx)])
    if step_x == 0:
        return lax.ppermute(value, "gy", [(s, (s + step_y) % ny) for s in range(ny)])
    pairs = [
        (i * ny + j, ((i + step_x) % nx) * ny + (j + step_y) % ny)
        for i in range(nx)
        for j in range(ny)
    ]
    return lax.ppermute(value, ("gx", "gy"), pairs)


PLACE = (8, 0, 3, 6, 7, 1, 2, 4, 5)


def fetch(sources, scratch, arrival):
    copies = [
        pltpu.make_async_copy(source, held, arrival.at[k])
        for k, (source, held) in enumerate(zip(sources, scratch))
    ]
    for copy in copies:
        copy.start()
    return copies


def block_rows(scratch, k):
    pos, vel, chg, rep, dis, inv = scratch[1:7]
    at = pl.ds(k, 1)
    return [pos[d, at, :] for d in range(3)] + [vel[d, at, :] for d in range(3)] + [
        ref[at, :] for ref in (chg, rep, dis, inv)
    ]


def pack_kernel(*refs):
    sources, parcels, scratch, tally, arrival = refs[:7], refs[7], refs[8:15], refs[15], refs[16]
    move = scratch[0]
    copies = fetch(sources, scratch, arrival)
    zero = jnp.zeros((8, BLOCK), jnp.float32)
    for p in range(8):
        for u in range(3):
            parcels[p, 8 * u : 8 * u + 8, :] = zero
    for code in range(9):
        tally[code] = 0
    for copy in copies:
        copy.wait()

    def one(k, carry):
        code = move[k]

        @pl.when(code != 0)
        def _():
            seen = tally[code]
            tally[code] = seen + 1
            to = tally[9 + code]
            slot = jnp.minimum(seen, 1) * 10
            for f, value in enumerate(block_rows(scratch, k)):
                parcels[to, pl.ds(slot + f, 1), :] = value

        return carry

    for code in range(1, 9):
        tally[9 + code] = PLACE[code]
    lax.fori_loop(0, NB, one, 0, unroll=4)
    for code in range(1, 9):
        step_x, step_y = OFFSETS[code]
        to = PLACE[code]
        for n in range(2):
            if step_x != 0:
                parcels[to, 10 * n : 10 * n + 1, :] = parcels[to, 10 * n : 10 * n + 1, :] - step_x * CELL
            if step_y != 0:
                parcels[to, 10 * n + 1 : 10 * n + 2, :] = parcels[to, 10 * n + 1 : 10 * n + 2, :] - step_y * CELL
        parcels[to, 20:21, :] = jnp.broadcast_to(tally[code], (1, BLOCK)).astype(jnp.float32)


def stay_kernel(*refs):
    sources, (stay, staying), scratch, arrival = refs[:7], refs[7:9], refs[9:16], refs[16]
    move = scratch[0]
    copies = fetch(sources, scratch, arrival)
    zero = jnp.zeros((8, BLOCK), jnp.float32)
    for f in range(10):
        for u in range(CAPACITY // 8):
            stay[f, 8 * u : 8 * u + 8, :] = zero
    for copy in copies:
        copy.wait()

    def one(k, kept):
        for f, value in enumerate(block_rows(scratch, k)):
            stay[f, pl.ds(kept, 1), :] = value
        return kept + jnp.where(move[k] == 0, 1, 0)

    kept = lax.fori_loop(0, NB, one, 0)
    for f in range(10):
        stay[f, pl.ds(kept, 1), :] = zero[0:1]
    staying[0] = kept


def turn_kernel(parcels, left, right, up, down):
    up[0], down[0] = parcels[6], parcels[7]
    up[1], down[1] = left[1], left[2]
    up[2], down[2] = right[1], right[2]


def arrive_kernel(staying, stay, *refs):
    left, right, up, down, coords, rest, held = refs
    parcels = [left.at[0], right.at[0], up.at[0], down.at[0], up.at[1], down.at[1], up.at[2], down.at[2]]
    for f in range(10):
        held[f, 0:CAPACITY, :] = stay[f]
    counts = jnp.concatenate([p[20:21, :] for p in parcels], axis=0).astype(jnp.int32)
    at = staying[0]
    for code in range(8):
        count = counts[code, 0]
        for n in range(2):
            for f in range(10):
                held[f, pl.ds(at, 1), :] = parcels[code][10 * n + f : 10 * n + f + 1, :]
            at = at + jnp.where(count > n, 1, 0)
    for f in range(10):
        held[f, pl.ds(at, 1), :] = jnp.zeros((1, BLOCK), jnp.float32)
    for k, f in enumerate((0, 1, 2, 6, 7, 8)):
        coords[k] = held[f, 0:CAPACITY, :]
    for k, f in enumerate((3, 4, 5, 9)):
        rest[k] = held[f, 0:CAPACITY, :]


def update_kernel(home, east, north, coords, rest, new_x, new_v, total):
    for d in range(3):
        force = home[d] + east[d] + north[d]
        fresh = rest[d] + TSTEP * rest[3] * force
        total[d] = force
        new_v[d] = fresh
        new_x[d] = coords[d] + TSTEP * fresh


def listed(b):
    return (b // 8) * 256 + (b % 8) * 16


def pair_kernel(tiles, home, east, north, corner, fh, fx, fn, zone, ac0, ac1, ac2, ibuf0, ibuf1, vbuf0, vbuf1, wbuf, *, T=2, mxu=True):
    acc=(ac0,ac1,ac2)
    sub = lax.broadcasted_iota(jnp.int32,(8,128),0)
    lane = lax.broadcasted_iota(jnp.int32,(8,128),1)
    rel = lane//4 - sub//4
    for c in range(16):
        wbuf[c]=jnp.where(rel==2*c,0.0,1.0)
    wbuf[16]=jnp.ones((8,128),jnp.float32)
    for z,(ref,sx,sy) in enumerate(((home,0.,0.),(east,2.,0.),(north,0.,2.),(corner,2.,2.))):
        for f in range(6):
            v = ref[f]
            if f==0 and sx: v=v+sx
            if f==1 and sy: v=v+sy
            zone[f, pl.ds(z*CAPACITY,CAPACITY), :] = v
    zero = jnp.zeros((8,128),jnp.float32)
    def clear(k,_):
        for u in range(16):
            for d in range(3):
                acc[d][pl.ds(pl.multiple_of(k*128,128)+8*u,8),:]=zero
        return 0
    lax.fori_loop(0,(4*CAPACITY)//16,clear,0)

    def row(f,j):
        return jnp.broadcast_to(zone[f, pl.ds(j,1), :],(8,128))
    SC=jnp.where(sub==4,12.0,jnp.where(sub==5,6.0,1.0)).astype(jnp.float32)
    kk=lax.broadcasted_iota(jnp.int32,(24,768),0); nn=lax.broadcasted_iota(jnp.int32,(24,768),1)
    pick=jnp.where(kk%8==nn//128,1.0,0.0).astype(jnp.bfloat16)

    def spread(b,ibuf):
        feat = jnp.concatenate([home[f, pl.ds(b,1), :] for f in range(6)]+[jnp.zeros((2,128),jnp.float32)],axis=0)*SC
        hi=feat.astype(jnp.bfloat16).astype(jnp.float32); r=feat-hi
        mid=r.astype(jnp.bfloat16).astype(jnp.float32); lo=r-mid
        ft=jnp.concatenate([hi,mid,lo],axis=0).T.astype(jnp.bfloat16)
        out=jnp.dot(ft,pick,preferred_element_type=jnp.float32)
        for f in range(6):
            for c in range(16): ibuf[f,c]=out[8*c:8*c+8,128*f:128*f+128]

    def settle(b,vbuf):
        tots=[]
        for c in range(16):
            tot=None
            for t in range(T):
                j8=pl.multiple_of(tiles[listed(b) + (128 * t + c)]*8,8)
                v=[vbuf[d,t,c] for d in range(3)]
                for d in range(3):
                    acc[d][pl.ds(j8,8),:]=acc[d][pl.ds(j8,8),:]+v[d]
                tot=v if tot is None else [p+q for p,q in zip(tot,v)]
            tots.append(tot)
        cc=[]
        for c in range(16):
            r=[jnp.sum(tots[c][d],axis=1,keepdims=True) for d in range(3)]
            cc.append(jnp.where(lane==0,r[0],jnp.where(lane==1,r[1],r[2])))
        m=jnp.concatenate(cc,axis=0)[:, :8].T
        for d in range(3):
            fh[d,pl.ds(b,1),:]=m[d:d+1]

    def block(b,ibuf,vbuf):
        for c in range(16):
            xi,yi,zi,qi,ai,bi=[ibuf[f,c] for f in range(6)]
            for t in range(T):
                j=tiles[listed(b) + (128 * t + c)]
                dx=xi-row(0,j); dy=yi-row(1,j); dz=zi-row(2,j)
                r2=dx*dx+dy*dy+dz*dz
                w=jnp.maximum(wbuf[jnp.where(j==b,c,16)]-r2,0.0)
                s=jnp.clip(r2,0.25,1.0)
                rs=lax.rsqrt(s)
                inv=rs*rs
                cube=inv*inv*inv
                h=RECIP_GAP[-1]
                for n in range(len(RECIP_GAP)-2,-1,-1):
                    h=h*s+RECIP_GAP[n]
                g=(qi*row(3,j))*(rs-h)+cube*((ai*row(4,j))*cube-bi*row(5,j))
                g=g*(inv*(w*w))
                vbuf[0,t,c]=g*dx
                vbuf[1,t,c]=g*dy
                vbuf[2,t,c]=g*dz

    spread(0,ibuf0)
    for d in range(3):
        for t in range(T):
            for c in range(16): vbuf1[d,t,c]=zero
    def two(k,_):
        b=2*k
        settle(jnp.maximum(b-1,0),vbuf1)
        spread(b+1,ibuf1)
        block(b,ibuf0,vbuf0)
        settle(b,vbuf0)
        spread(jnp.minimum(b+2,CAPACITY-1),ibuf0)
        block(b+1,ibuf1,vbuf1)
        return 0
    lax.fori_loop(0,CAPACITY//2,two,0)
    settle(CAPACITY-1,vbuf1)
    for d in range(3):
        for z,(ref,o) in enumerate(((fh,0),(fx,0),(fn,0),(fx,3))):
            def red(k,_):
                for u in range(3):
                    k8=pl.multiple_of(k*24+8*u,8)
                    r=[acc[d][pl.ds((z*CAPACITY+k8)*8+q,8,stride=8),:] for q in range(8)]
                    r=((r[0]+r[1])+(r[2]+r[3]))+((r[4]+r[5])+(r[6]+r[7]))
                    if z==0: ref[o+d,pl.ds(k8,8),:]=ref[o+d,pl.ds(k8,8),:]-r
                    else: ref[o+d,pl.ds(k8,8),:]=-r
                return 0
            lax.fori_loop(0,CAPACITY//24,red,0)


VM = pl.BlockSpec(memory_space=pltpu.VMEM)
SM = pl.BlockSpec(memory_space=pltpu.SMEM)
HBM = pl.BlockSpec(memory_space=pltpu.HBM)
PARAMS = pltpu.CompilerParams(vmem_limit_bytes=48 * 1024 * 1024)
WIDE = pltpu.CompilerParams(vmem_limit_bytes=56 * 1024 * 1024)


def planes(count, rows=CAPACITY):
    return jax.ShapeDtypeStruct((count, rows, BLOCK), jnp.float32)


def body(positions, velocities, charges, repel_root, disperse_root, inverse_mass, move, tiles):
    inputs = (
        move.reshape(NB),
        positions.reshape(3, NB, BLOCK),
        velocities.reshape(3, NB, BLOCK),
        charges.reshape(NB, BLOCK),
        repel_root.reshape(NB, BLOCK),
        disperse_root.reshape(NB, BLOCK),
        inverse_mass.reshape(NB, BLOCK),
    )
    held = (
        [pltpu.SMEM((NB,), jnp.int32)]
        + [pltpu.VMEM((3, NB, BLOCK), jnp.float32)] * 2
        + [pltpu.VMEM((NB, BLOCK), jnp.float32)] * 4
    )
    parcels = pl.pallas_call(
        pack_kernel,
        out_shape=planes(8, 24),
        in_specs=[HBM] * 7,
        out_specs=VM,
        scratch_shapes=held + [pltpu.SMEM((18,), jnp.int32), pltpu.SemaphoreType.DMA((7,))],
        compiler_params=WIDE,
        name="pack",
    )(*inputs)
    left = passed_along(parcels[0:3], 1, 0)
    right = passed_along(parcels[3:6], -1, 0)
    stay, staying = pl.pallas_call(
        stay_kernel,
        out_shape=(planes(10), jax.ShapeDtypeStruct((1,), jnp.int32)),
        in_specs=[HBM] * 7,
        out_specs=(VM, SM),
        scratch_shapes=held + [pltpu.SemaphoreType.DMA((7,))],
        compiler_params=WIDE,
        cost_estimate=pl.CostEstimate(flops=0, bytes_accessed=6_000_000, transcendentals=0),
        name="stay",
    )(*inputs)
    up, down = pl.pallas_call(
        turn_kernel,
        out_shape=(planes(3, 24),) * 2,
        in_specs=[VM] * 3,
        out_specs=(VM,) * 2,
        compiler_params=PARAMS,
        name="turn",
    )(parcels, left, right)
    up = passed_along(up, 0, 1)
    down = passed_along(down, 0, -1)
    coords, rest = pl.pallas_call(
        arrive_kernel,
        out_shape=(planes(6), planes(4)),
        in_specs=[SM] + [VM] * 5,
        out_specs=(VM, VM),
        scratch_shapes=[pltpu.VMEM((10, CAPACITY + 8, BLOCK), jnp.float32)],
        compiler_params=PARAMS,
        name="arrive",
    )(staying, stay, left, right, up, down)
    east = passed_along(coords, -1, 0)
    north = passed_along(coords, 0, -1)
    corner = passed_along(north, -1, 0)
    on_home, on_x, on_north = pl.pallas_call(
        pair_kernel,
        out_shape=(planes(3), planes(6), planes(3)),
        in_specs=[SM] + [VM] * 4,
        out_specs=(VM,) * 3,
        scratch_shapes=[pltpu.VMEM((6,4 * CAPACITY,128),jnp.float32)]+[pltpu.VMEM((4 * CAPACITY*8,128),jnp.float32)]*3+[pltpu.VMEM((6,16,8,128),jnp.float32)]*2+[pltpu.VMEM((3,2,16,8,128),jnp.float32)]*2+[pltpu.VMEM((17,8,128),jnp.float32)],
        compiler_params=PARAMS,
        name="pair",
    )(tiles.reshape(18, 128, 2).transpose(0, 2, 1).reshape(-1), coords, east, north, corner)
    from_x = passed_along(on_x, 1, 0)
    from_north = passed_along(on_north + from_x[3:6], 0, 1)
    out = pl.pallas_call(
        update_kernel,
        out_shape=(planes(3),) * 3,
        in_specs=[VM] * 5,
        out_specs=(VM,) * 3,
        compiler_params=PARAMS,
        name="update",
    )(on_home, from_x, from_north, coords, rest)
    return tuple(value.reshape(3, 1, 1, CAPACITY * BLOCK) for value in out)


def solution(mesh):
    vector = P(None, "gx", "gy", None)
    scalar = P("gx", "gy", None)
    return jax.shard_map(
        body,
        mesh=mesh,
        in_specs=(vector, vector) + (scalar,) * 5 + (P("gx", "gy", None, None),),
        out_specs=(vector,) * 3,
        check_vma=False,
    )
```

```python
import functools

import jax
import jax.numpy as jnp
from jax import lax
from jax.experimental import pallas as pl
from jax.experimental.pallas import tpu as pltpu
from jax.sharding import PartitionSpec as P

BLOCK = 128
NB = 128
CAPACITY = 144
CELL = 2.0
TSTEP = 0.05
OFFSETS = ((0, 0), (1, 0), (-1, 0), (0, 1), (0, -1), (1, 1), (1, -1), (-1, 1), (-1, -1))
LOG2E = 1.4426950408889634
HALFC = 1.1283791670955126


def passed_along(value, step_x, step_y):
    nx, ny = lax.axis_size("gx"), lax.axis_size("gy")
    if step_y == 0:
        return lax.ppermute(value, "gx", [(s, (s + step_x) % nx) for s in range(nx)])
    if step_x == 0:
        return lax.ppermute(value, "gy", [(s, (s + step_y) % ny) for s in range(ny)])
    pairs = [
        (i * ny + j, ((i + step_x) % nx) * ny + (j + step_y) % ny)
        for i in range(nx)
        for j in range(ny)
    ]
    return lax.ppermute(value, ("gx", "gy"), pairs)


PLACE = (8, 0, 3, 6, 7, 1, 2, 4, 5)


def fetch(sources, scratch, arrival):
    copies = [
        pltpu.make_async_copy(source, held, arrival.at[k])
        for k, (source, held) in enumerate(zip(sources, scratch))
    ]
    for copy in copies:
        copy.start()
    return copies


def block_rows(scratch, k):
    pos, vel, chg, rep, dis, inv = scratch[1:7]
    at = pl.ds(k, 1)
    return [pos[d, at, :] for d in range(3)] + [vel[d, at, :] for d in range(3)] + [
        ref[at, :] for ref in (chg, rep, dis, inv)
    ]


def pack_kernel(*refs):
    sources, outs, scratch, tally, arrival = refs[:7], refs[7:10], refs[10:17], refs[17], refs[18]
    parcels = refs[19]
    move = scratch[0]
    copies = fetch(sources, scratch, arrival)
    zero = jnp.zeros((8, BLOCK), jnp.float32)
    for p in range(8):
        for u in range(3):
            parcels[p, 8 * u : 8 * u + 8, :] = zero
    for code in range(9):
        tally[code] = 0
    for copy in copies:
        copy.wait()

    def one(k, carry):
        code = move[k]

        @pl.when(code != 0)
        def _():
            seen = tally[code]
            tally[code] = seen + 1
            to = tally[9 + code]
            slot = jnp.minimum(seen, 1) * 10
            for f, value in enumerate(block_rows(scratch, k)):
                parcels[to, pl.ds(slot + f, 1), :] = value

        return carry

    for code in range(1, 9):
        tally[9 + code] = PLACE[code]
    lax.fori_loop(0, NB, one, 0, unroll=4)
    for code in range(1, 9):
        step_x, step_y = OFFSETS[code]
        to = PLACE[code]
        for n in range(2):
            if step_x != 0:
                parcels[to, 10 * n : 10 * n + 1, :] = parcels[to, 10 * n : 10 * n + 1, :] - step_x * CELL
            if step_y != 0:
                parcels[to, 10 * n + 1 : 10 * n + 2, :] = parcels[to, 10 * n + 1 : 10 * n + 2, :] - step_y * CELL
        parcels[to, 20:21, :] = jnp.broadcast_to(tally[code], (1, BLOCK)).astype(jnp.float32)
    for ref, first in zip(outs, (0, 3, 6)):
        for p in range(ref.shape[0]):
            ref[p] = parcels[first + p]


def stay_kernel(*refs):
    sources, (stay, staying), scratch, arrival = refs[:7], refs[7:9], refs[9:16], refs[16]
    move = scratch[0]
    copies = fetch(sources, scratch, arrival)
    zero = jnp.zeros((8, BLOCK), jnp.float32)
    for f in range(10):
        for u in range(CAPACITY // 8):
            stay[f, 8 * u : 8 * u + 8, :] = zero
    for copy in copies:
        copy.wait()

    def one(k, kept):
        for f, value in enumerate(block_rows(scratch, k)):
            stay[f, pl.ds(kept, 1), :] = value
        return kept + jnp.where(move[k] == 0, 1, 0)

    kept = lax.fori_loop(0, NB, one, 0)
    for f in range(10):
        stay[f, pl.ds(kept, 1), :] = zero[0:1]
    staying[0] = kept


def turn_kernel(staying, own, left, right, up, down):
    up[0], down[0] = own[0], own[1]
    up[1], down[1] = left[1], left[2]
    up[2], down[2] = right[1], right[2]


def arrive_kernel(staying, stay, *refs):
    left, right, up, down, coords, rest, held = refs
    parcels = [left.at[0], right.at[0], up.at[0], down.at[0], up.at[1], down.at[1], up.at[2], down.at[2]]
    for f in range(10):
        held[f, 0:CAPACITY, :] = stay[f]
    counts = jnp.concatenate([p[20:21, :] for p in parcels], axis=0).astype(jnp.int32)
    at = staying[0]
    for code in range(8):
        count = counts[code, 0]
        for n in range(2):
            for f in range(10):
                held[f, pl.ds(at, 1), :] = parcels[code][10 * n + f : 10 * n + f + 1, :]
            at = at + jnp.where(count > n, 1, 0)
    for f in range(10):
        held[f, pl.ds(at, 1), :] = jnp.zeros((1, BLOCK), jnp.float32)
    for k, f in enumerate((0, 1, 2, 6, 7, 8)):
        coords[k] = held[f, 0:CAPACITY, :]
    for k, f in enumerate((3, 4, 5, 9)):
        rest[k] = held[f, 0:CAPACITY, :]


def update_kernel(home, east, north, coords, rest, new_x, new_v, total):
    for d in range(3):
        force = home[d] + east[d] + north[d]
        fresh = rest[d] + TSTEP * rest[3] * force
        total[d] = force
        new_v[d] = fresh
        new_x[d] = coords[d] + TSTEP * fresh


def listed(b):
    return (b // 8) * 256 + (b % 8) * 16


def pair_kernel(tiles, home, east, north, corner, fh, fe, fn, fc, zone, ac0, ac1, ac2, ibuf0, ibuf1, vbuf0, vbuf1, wbuf, *, T=2, mxu=True):
    acc=(ac0,ac1,ac2)
    sub = lax.broadcasted_iota(jnp.int32,(8,128),0)
    lane = lax.broadcasted_iota(jnp.int32,(8,128),1)
    rel = lane//4 - sub//4
    for c in range(16):
        wbuf[c]=jnp.where(rel==2*c,0.0,4.0)
    wbuf[16]=jnp.full((8,128),4.0,jnp.float32)
    for z,(ref,sx,sy) in enumerate(((home,0.,0.),(east,2.,0.),(north,0.,2.),(corner,2.,2.))):
        for f in range(6):
            v = ref[f]
            if f==0 and sx: v=v+sx
            if f==1 and sy: v=v+sy
            if f<3: v=v*2.0
            zone[f, pl.ds(z*CAPACITY,CAPACITY), :] = v
    zero = jnp.zeros((8,128),jnp.float32)
    def clear(k,_):
        for u in range(16):
            for d in range(3):
                acc[d][pl.ds(pl.multiple_of(k*128,128)+8*u,8),:]=zero
        return 0
    lax.fori_loop(0,(4*CAPACITY)//16,clear,0)

    def row(f,j):
        return jnp.broadcast_to(zone[f, pl.ds(j,1), :],(8,128))
    SC=jnp.where(sub==4,6144.0,jnp.where(sub==5,48.0,jnp.where(sub==3,0.25,2.0))).astype(jnp.float32)
    kk=lax.broadcasted_iota(jnp.int32,(24,768),0); nn=lax.broadcasted_iota(jnp.int32,(24,768),1)
    pick=jnp.where(kk%8==nn//128,1.0,0.0).astype(jnp.bfloat16)

    def spread(b,ibuf):
        feat = jnp.concatenate([home[f, pl.ds(b,1), :] for f in range(6)]+[jnp.zeros((2,128),jnp.float32)],axis=0)*SC
        hi=feat.astype(jnp.bfloat16).astype(jnp.float32); r=feat-hi
        mid=r.astype(jnp.bfloat16).astype(jnp.float32); lo=r-mid
        ft=jnp.concatenate([hi,mid,lo],axis=0).T.astype(jnp.bfloat16)
        out=jnp.dot(ft,pick,preferred_element_type=jnp.float32)
        for f in range(6):
            for c in range(16): ibuf[f,c]=out[8*c:8*c+8,128*f:128*f+128]

    def settle(b,vbuf):
        tots=[]
        for c in range(16):
            tot=None
            for t in range(T):
                j8=pl.multiple_of(tiles[listed(b) + (128 * t + c)]*8,8)
                v=[vbuf[d,t,c] for d in range(3)]
                for d in range(3):
                    acc[d][pl.ds(j8,8),:]=acc[d][pl.ds(j8,8),:]+v[d]
                tot=v if tot is None else [p+q for p,q in zip(tot,v)]
            tots.append(tot)
        cc=[]
        for c in range(16):
            r=[jnp.sum(tots[c][d],axis=1,keepdims=True) for d in range(3)]
            cc.append(jnp.where(lane==0,r[0],jnp.where(lane==1,r[1],r[2])))
        m=jnp.concatenate(cc,axis=0)[:, :8].T
        for d in range(3):
            fh[d,pl.ds(b,1),:]=m[d:d+1]

    def block(b,ibuf,vbuf):
        for c in range(16):
            xi,yi,zi,qi,ai,bi=[ibuf[f,c] for f in range(6)]
            for t in range(T):
                j=tiles[listed(b) + (128 * t + c)]
                dx=xi-row(0,j); dy=yi-row(1,j); dz=zi-row(2,j)
                r2=dx*dx+dy*dy+dz*dz
                w=jnp.maximum(wbuf[jnp.where(j==b,c,16)]-r2,0.0)
                s=jnp.clip(r2,1.0,4.0)
                rs=lax.rsqrt(s)
                inv=rs*rs
                cube=inv*inv*inv
                ew=jnp.exp2(s*-LOG2E)
                kc=(1.0-lax.erf(s*rs))*rs+ew*HALFC
                g=(qi*row(3,j))*kc+cube*((ai*row(4,j))*cube-bi*row(5,j))
                g=g*(inv*(w*w))
                vbuf[0,t,c]=g*dx
                vbuf[1,t,c]=g*dy
                vbuf[2,t,c]=g*dz

    spread(0,ibuf0)
    for d in range(3):
        for t in range(T):
            for c in range(16): vbuf1[d,t,c]=zero
    ib=(ibuf0,ibuf0); vb=(vbuf0,vbuf1)
    def some(k,_):
        b=4*k
        for n in range(4):
            settle(jnp.maximum(b+n-1,0),vb[(n+1)%2])
            pass
            block(b+n,ib[n%2],vb[n%2])
            spread(jnp.minimum(b+n+1,CAPACITY-1),ib[(n+1)%2])
        return 0
    lax.fori_loop(0,CAPACITY//4,some,0)
    settle(CAPACITY-1,vb[1])
    for d in range(3):
        for z,ref in enumerate((fh,fe,fn,fc)):
            def red(k,_):
                for u in range(3):
                    k8=pl.multiple_of(k*24+8*u,8)
                    r=[acc[d][pl.ds((z*CAPACITY+k8)*8+q,8,stride=8),:] for q in range(8)]
                    r=((r[0]+r[1])+(r[2]+r[3]))+((r[4]+r[5])+(r[6]+r[7]))
                    if z==0: ref[d,pl.ds(k8,8),:]=ref[d,pl.ds(k8,8),:]-r
                    else: ref[d,pl.ds(k8,8),:]=-r
                return 0
            lax.fori_loop(0,CAPACITY//24,red,0)

VM = pl.BlockSpec(memory_space=pltpu.VMEM)
SM = pl.BlockSpec(memory_space=pltpu.SMEM)
HBM = pl.BlockSpec(memory_space=pltpu.HBM)
PARAMS = pltpu.CompilerParams(vmem_limit_bytes=48 * 1024 * 1024)
WIDE = pltpu.CompilerParams(vmem_limit_bytes=56 * 1024 * 1024)


def planes(count, rows=CAPACITY):
    return jax.ShapeDtypeStruct((count, rows, BLOCK), jnp.float32)


def body(positions, velocities, charges, repel_root, disperse_root, inverse_mass, move, tiles):
    inputs = (
        move.reshape(NB),
        positions.reshape(3, NB, BLOCK),
        velocities.reshape(3, NB, BLOCK),
        charges.reshape(NB, BLOCK),
        repel_root.reshape(NB, BLOCK),
        disperse_root.reshape(NB, BLOCK),
        inverse_mass.reshape(NB, BLOCK),
    )
    held = (
        [pltpu.SMEM((NB,), jnp.int32)]
        + [pltpu.VMEM((3, NB, BLOCK), jnp.float32)] * 2
        + [pltpu.VMEM((NB, BLOCK), jnp.float32)] * 4
    )
    going_up_x, going_down_x, own = pl.pallas_call(
        pack_kernel,
        out_shape=(planes(3, 24), planes(3, 24), planes(2, 24)),
        in_specs=[HBM] * 7,
        out_specs=(VM,) * 3,
        scratch_shapes=held
        + [pltpu.SMEM((18,), jnp.int32), pltpu.SemaphoreType.DMA((7,)), pltpu.VMEM((8, 24, BLOCK), jnp.float32)],
        compiler_params=WIDE,
        name="pack",
    )(*inputs)
    left = passed_along(going_up_x, 1, 0)
    right = passed_along(going_down_x, -1, 0)
    stay, staying = pl.pallas_call(
        stay_kernel,
        out_shape=(planes(10), jax.ShapeDtypeStruct((1,), jnp.int32)),
        in_specs=[HBM] * 7,
        out_specs=(VM, SM),
        scratch_shapes=held + [pltpu.SemaphoreType.DMA((7,))],
        compiler_params=WIDE,
        cost_estimate=pl.CostEstimate(flops=0, bytes_accessed=6_000_000, transcendentals=0),
        name="stay",
    )(*inputs)
    up, down = pl.pallas_call(
        turn_kernel,
        out_shape=(planes(3, 24),) * 2,
        in_specs=[SM] + [VM] * 3,
        out_specs=(VM,) * 2,
        compiler_params=PARAMS,
        name="turn",
    )(staying, own, left, right)
    up = passed_along(up, 0, 1)
    down = passed_along(down, 0, -1)
    coords, rest = pl.pallas_call(
        arrive_kernel,
        out_shape=(planes(6), planes(4)),
        in_specs=[SM] + [VM] * 5,
        out_specs=(VM, VM),
        scratch_shapes=[pltpu.VMEM((10, CAPACITY + 8, BLOCK), jnp.float32)],
        compiler_params=PARAMS,
        name="arrive",
    )(staying, stay, left, right, up, down)
    east = passed_along(coords, -1, 0)
    north = passed_along(coords, 0, -1)
    corner = passed_along(north, -1, 0)
    on_home, on_east, on_north, on_corner = pl.pallas_call(
        pair_kernel,
        out_shape=(planes(3),) * 4,
        in_specs=[SM] + [VM] * 4,
        out_specs=(VM,) * 4,
        scratch_shapes=[pltpu.VMEM((6,4 * CAPACITY,128),jnp.float32)]+[pltpu.VMEM((4 * CAPACITY*8,128),jnp.float32)]*3+[pltpu.VMEM((6,16,8,128),jnp.float32)]*2+[pltpu.VMEM((3,2,16,8,128),jnp.float32)]*2+[pltpu.VMEM((17,8,128),jnp.float32)],
        compiler_params=PARAMS,
        name="pair",
    )(tiles.reshape(18, 128, 2).transpose(0, 2, 1).reshape(-1), coords, east, north, corner)
    from_corner = passed_along(on_corner, 1, 0)
    from_east = passed_along(on_east, 1, 0)
    from_north = passed_along(on_north + from_corner, 0, 1)
    out = pl.pallas_call(
        update_kernel,
        out_shape=(planes(3),) * 3,
        in_specs=[VM] * 5,
        out_specs=(VM,) * 3,
        compiler_params=PARAMS,
        name="update",
    )(on_home, from_east, from_north, coords, rest)
    return tuple(value.reshape(3, 1, 1, CAPACITY * BLOCK) for value in out)


def solution(mesh):
    vector = P(None, "gx", "gy", None)
    scalar = P("gx", "gy", None)
    return jax.shard_map(
        body,
        mesh=mesh,
        in_specs=(vector, vector) + (scalar,) * 5 + (P("gx", "gy", None, None),),
        out_specs=(vector,) * 3,
        check_vma=False,
    )
```

```python
import functools

import jax
import jax.numpy as jnp
from jax import lax
from jax.experimental import pallas as pl
from jax.experimental.pallas import tpu as pltpu
from jax.sharding import PartitionSpec as P

BLOCK = 128
NB = 128
CAPACITY = 144
CELL = 2.0
TSTEP = 0.05
OFFSETS = ((0, 0), (1, 0), (-1, 0), (0, 1), (0, -1), (1, 1), (1, -1), (-1, 1), (-1, -1))
LOG2E = 1.4426950408889634
HALFC = 1.1283791670955126


def passed_along(value, step_x, step_y):
    nx, ny = lax.axis_size("gx"), lax.axis_size("gy")
    if step_y == 0:
        return lax.ppermute(value, "gx", [(s, (s + step_x) % nx) for s in range(nx)])
    if step_x == 0:
        return lax.ppermute(value, "gy", [(s, (s + step_y) % ny) for s in range(ny)])
    pairs = [
        (i * ny + j, ((i + step_x) % nx) * ny + (j + step_y) % ny)
        for i in range(nx)
        for j in range(ny)
    ]
    return lax.ppermute(value, ("gx", "gy"), pairs)


PLACE = (8, 0, 3, 6, 7, 1, 2, 4, 5)


def sent(value, step_x, step_y, parity):
    nx, ny = lax.axis_size("gx"), lax.axis_size("gy")
    if step_y == 0:
        return lax.ppermute(value, "gx", [(s, (s + step_x) % nx) for s in range(nx) if s % 2 == parity])
    pairs = [
        (i * ny + j, ((i + step_x) % nx) * ny + (j + step_y) % ny)
        for i in range(nx)
        for j in range(ny)
        if i % 2 == parity
    ]
    return lax.ppermute(value, ("gx", "gy"), pairs)


def fetch(sources, scratch, arrival):
    copies = [
        pltpu.make_async_copy(source, held, arrival.at[k])
        for k, (source, held) in enumerate(zip(sources, scratch))
    ]
    for copy in copies:
        copy.start()
    return copies


def block_rows(scratch, k):
    pos, vel, chg, rep, dis, inv = scratch[1:7]
    at = pl.ds(k, 1)
    return [pos[d, at, :] for d in range(3)] + [vel[d, at, :] for d in range(3)] + [
        ref[at, :] for ref in (chg, rep, dis, inv)
    ]


def pack_kernel(*refs):
    sources, outs, scratch, tally, arrival = refs[:7], refs[7:10], refs[10:17], refs[17], refs[18]
    parcels = refs[19]
    move = scratch[0]
    copies = fetch(sources, scratch, arrival)
    zero = jnp.zeros((8, BLOCK), jnp.float32)
    for p in range(8):
        for u in range(3):
            parcels[p, 8 * u : 8 * u + 8, :] = zero
    for code in range(9):
        tally[code] = 0
    for copy in copies:
        copy.wait()

    def one(k, carry):
        code = move[k]

        @pl.when(code != 0)
        def _():
            seen = tally[code]
            tally[code] = seen + 1
            to = tally[9 + code]
            slot = jnp.minimum(seen, 1) * 10
            for f, value in enumerate(block_rows(scratch, k)):
                parcels[to, pl.ds(slot + f, 1), :] = value

        return carry

    for code in range(1, 9):
        tally[9 + code] = PLACE[code]
    lax.fori_loop(0, NB, one, 0, unroll=4)
    for code in range(1, 9):
        step_x, step_y = OFFSETS[code]
        to = PLACE[code]
        for n in range(2):
            if step_x != 0:
                parcels[to, 10 * n : 10 * n + 1, :] = parcels[to, 10 * n : 10 * n + 1, :] - step_x * CELL
            if step_y != 0:
                parcels[to, 10 * n + 1 : 10 * n + 2, :] = parcels[to, 10 * n + 1 : 10 * n + 2, :] - step_y * CELL
        parcels[to, 20:21, :] = jnp.broadcast_to(tally[code], (1, BLOCK)).astype(jnp.float32)
    for ref, first in zip(outs, (0, 3, 6)):
        for p in range(ref.shape[0]):
            ref[p] = parcels[first + p]


def stay_kernel(*refs):
    sources, (stay, staying), scratch, arrival = refs[:7], refs[7:9], refs[9:16], refs[16]
    move = scratch[0]
    copies = fetch(sources, scratch, arrival)
    zero = jnp.zeros((8, BLOCK), jnp.float32)
    for f in range(10):
        for u in range(CAPACITY // 8):
            stay[f, 8 * u : 8 * u + 8, :] = zero
    for copy in copies:
        copy.wait()

    def one(k, kept):
        for f, value in enumerate(block_rows(scratch, k)):
            stay[f, pl.ds(kept, 1), :] = value
        return kept + jnp.where(move[k] == 0, 1, 0)

    kept = lax.fori_loop(0, NB, one, 0)
    for f in range(10):
        stay[f, pl.ds(kept, 1), :] = zero[0:1]
    staying[0] = kept


def turn_kernel(staying, own, left, right, up, down):
    up[0], down[0] = own[0], own[1]
    up[1], down[1] = left[1], left[2]
    up[2], down[2] = right[1], right[2]


def arrive_kernel(staying, stay, *refs):
    left, right, up, down, coords, rest, held = refs
    parcels = [left.at[0], right.at[0], up.at[0], down.at[0], up.at[1], down.at[1], up.at[2], down.at[2]]
    for f in range(10):
        held[f, 0:CAPACITY, :] = stay[f]
    counts = jnp.concatenate([p[20:21, :] for p in parcels], axis=0).astype(jnp.int32)
    at = staying[0]
    for code in range(8):
        count = counts[code, 0]
        for n in range(2):
            for f in range(10):
                held[f, pl.ds(at, 1), :] = parcels[code][10 * n + f : 10 * n + f + 1, :]
            at = at + jnp.where(count > n, 1, 0)
    for f in range(10):
        held[f, pl.ds(at, 1), :] = jnp.zeros((1, BLOCK), jnp.float32)
    for k, f in enumerate((0, 1, 2, 6, 7, 8)):
        coords[k] = held[f, 0:CAPACITY, :]
    for k, f in enumerate((3, 4, 5, 9)):
        rest[k] = held[f, 0:CAPACITY, :]


def update_kernel(home, east, north, far, coords, rest, new_x, new_v, total):
    for d in range(3):
        force = home[d] + east[d] + north[d] + far[d]
        fresh = rest[d] + TSTEP * rest[3] * force
        total[d] = force
        new_v[d] = fresh
        new_x[d] = coords[d] + TSTEP * fresh


def listed(b):
    return (b // 8) * 256 + (b % 8) * 16


def pair_kernel(tiles, home, east, north, near, far, fh, fe, fn, fc, zone, ac0, ac1, ac2, ibuf0, ibuf1, vbuf0, vbuf1, wbuf, *, T=2, mxu=True):
    acc=(ac0,ac1,ac2)
    sub = lax.broadcasted_iota(jnp.int32,(8,128),0)
    lane = lax.broadcasted_iota(jnp.int32,(8,128),1)
    rel = lane//4 - sub//4
    for c in range(16):
        wbuf[c]=jnp.where(rel==2*c,0.0,4.0)
    wbuf[16]=jnp.full((8,128),4.0,jnp.float32)
    for z,(ref,sx,sy) in enumerate(((home,0.,0.),(east,2.,0.),(north,0.,2.),(near,2.,2.))):
        for f in range(6):
            v = ref[f]+far[f] if z==3 else ref[f]
            if f==0 and sx: v=v+sx
            if f==1 and sy: v=v+sy
            if f<3: v=v*2.0
            zone[f, pl.ds(z*CAPACITY,CAPACITY), :] = v
    zero = jnp.zeros((8,128),jnp.float32)
    def clear(k,_):
        for u in range(16):
            for d in range(3):
                acc[d][pl.ds(pl.multiple_of(k*128,128)+8*u,8),:]=zero
        return 0
    lax.fori_loop(0,(4*CAPACITY)//16,clear,0)

    def row(f,j):
        return jnp.broadcast_to(zone[f, pl.ds(j,1), :],(8,128))
    SC=jnp.where(sub==4,6144.0,jnp.where(sub==5,48.0,jnp.where(sub==3,0.25,2.0))).astype(jnp.float32)
    kk=lax.broadcasted_iota(jnp.int32,(24,768),0); nn=lax.broadcasted_iota(jnp.int32,(24,768),1)
    pick=jnp.where(kk%8==nn//128,1.0,0.0).astype(jnp.bfloat16)

    def spread(b,ibuf):
        feat = jnp.concatenate([home[f, pl.ds(b,1), :] for f in range(6)]+[jnp.zeros((2,128),jnp.float32)],axis=0)*SC
        hi=feat.astype(jnp.bfloat16).astype(jnp.float32); r=feat-hi
        mid=r.astype(jnp.bfloat16).astype(jnp.float32); lo=r-mid
        ft=jnp.concatenate([hi,mid,lo],axis=0).T.astype(jnp.bfloat16)
        out=jnp.dot(ft,pick,preferred_element_type=jnp.float32)
        for f in range(6):
            for c in range(16): ibuf[f,c]=out[8*c:8*c+8,128*f:128*f+128]

    def settle(b,vbuf):
        tots=[]
        for c in range(16):
            tot=None
            for t in range(T):
                j8=pl.multiple_of(tiles[listed(b) + (128 * t + c)]*8,8)
                v=[vbuf[d,t,c] for d in range(3)]
                for d in range(3):
                    acc[d][pl.ds(j8,8),:]=acc[d][pl.ds(j8,8),:]+v[d]
                tot=v if tot is None else [p+q for p,q in zip(tot,v)]
            tots.append(tot)
        cc=[]
        for c in range(16):
            r=[jnp.sum(tots[c][d],axis=1,keepdims=True) for d in range(3)]
            cc.append(jnp.where(lane==0,r[0],jnp.where(lane==1,r[1],r[2])))
        m=jnp.concatenate(cc,axis=0)[:, :8].T
        for d in range(3):
            fh[d,pl.ds(b,1),:]=m[d:d+1]

    def block(b,ibuf,vbuf):
        for c in range(16):
            xi,yi,zi,qi,ai,bi=[ibuf[f,c] for f in range(6)]
            for t in range(T):
                j=tiles[listed(b) + (128 * t + c)]
                dx=xi-row(0,j); dy=yi-row(1,j); dz=zi-row(2,j)
                r2=dx*dx+dy*dy+dz*dz
                w=jnp.maximum(wbuf[jnp.where(j==b,c,16)]-r2,0.0)
                s=jnp.clip(r2,1.0,4.0)
                rs=lax.rsqrt(s)
                inv=rs*rs
                cube=inv*inv*inv
                ew=jnp.exp2(s*-LOG2E)
                kc=(1.0-lax.erf(s*rs))*rs+ew*HALFC
                g=(qi*row(3,j))*kc+cube*((ai*row(4,j))*cube-bi*row(5,j))
                g=g*(inv*(w*w))
                vbuf[0,t,c]=g*dx
                vbuf[1,t,c]=g*dy
                vbuf[2,t,c]=g*dz

    spread(0,ibuf0)
    for d in range(3):
        for t in range(T):
            for c in range(16): vbuf1[d,t,c]=zero
    ib=(ibuf0,ibuf0); vb=(vbuf0,vbuf1)
    def some(k,_):
        b=4*k
        for n in range(4):
            settle(jnp.maximum(b+n-1,0),vb[(n+1)%2])
            pass
            block(b+n,ib[n%2],vb[n%2])
            spread(jnp.minimum(b+n+1,CAPACITY-1),ib[(n+1)%2])
        return 0
    lax.fori_loop(0,CAPACITY//4,some,0)
    settle(CAPACITY-1,vb[1])
    for d in range(3):
        for z,ref in enumerate((fh,fe,fn,fc)):
            def red(k,_):
                for u in range(3):
                    k8=pl.multiple_of(k*24+8*u,8)
                    r=[acc[d][pl.ds((z*CAPACITY+k8)*8+q,8,stride=8),:] for q in range(8)]
                    r=((r[0]+r[1])+(r[2]+r[3]))+((r[4]+r[5])+(r[6]+r[7]))
                    if z==0: ref[d,pl.ds(k8,8),:]=ref[d,pl.ds(k8,8),:]-r
                    else: ref[d,pl.ds(k8,8),:]=-r
                return 0
            lax.fori_loop(0,CAPACITY//24,red,0)

VM = pl.BlockSpec(memory_space=pltpu.VMEM)
SM = pl.BlockSpec(memory_space=pltpu.SMEM)
HBM = pl.BlockSpec(memory_space=pltpu.HBM)
PARAMS = pltpu.CompilerParams(vmem_limit_bytes=48 * 1024 * 1024)
WIDE = pltpu.CompilerParams(vmem_limit_bytes=56 * 1024 * 1024)


def planes(count, rows=CAPACITY):
    return jax.ShapeDtypeStruct((count, rows, BLOCK), jnp.float32)


def body(positions, velocities, charges, repel_root, disperse_root, inverse_mass, move, tiles):
    inputs = (
        move.reshape(NB),
        positions.reshape(3, NB, BLOCK),
        velocities.reshape(3, NB, BLOCK),
        charges.reshape(NB, BLOCK),
        repel_root.reshape(NB, BLOCK),
        disperse_root.reshape(NB, BLOCK),
        inverse_mass.reshape(NB, BLOCK),
    )
    held = (
        [pltpu.SMEM((NB,), jnp.int32)]
        + [pltpu.VMEM((3, NB, BLOCK), jnp.float32)] * 2
        + [pltpu.VMEM((NB, BLOCK), jnp.float32)] * 4
    )
    going_up_x, going_down_x, own = pl.pallas_call(
        pack_kernel,
        out_shape=(planes(3, 24), planes(3, 24), planes(2, 24)),
        in_specs=[HBM] * 7,
        out_specs=(VM,) * 3,
        scratch_shapes=held
        + [pltpu.SMEM((18,), jnp.int32), pltpu.SemaphoreType.DMA((7,)), pltpu.VMEM((8, 24, BLOCK), jnp.float32)],
        compiler_params=WIDE,
        name="pack",
    )(*inputs)
    left = passed_along(going_up_x, 1, 0)
    right = passed_along(going_down_x, -1, 0)
    stay, staying = pl.pallas_call(
        stay_kernel,
        out_shape=(planes(10), jax.ShapeDtypeStruct((1,), jnp.int32)),
        in_specs=[HBM] * 7,
        out_specs=(VM, SM),
        scratch_shapes=held + [pltpu.SemaphoreType.DMA((7,))],
        compiler_params=WIDE,
        cost_estimate=pl.CostEstimate(flops=0, bytes_accessed=6_000_000, transcendentals=0),
        name="stay",
    )(*inputs)
    up, down = pl.pallas_call(
        turn_kernel,
        out_shape=(planes(3, 24),) * 2,
        in_specs=[SM] + [VM] * 3,
        out_specs=(VM,) * 2,
        compiler_params=PARAMS,
        name="turn",
    )(staying, own, left, right)
    up = passed_along(up, 0, 1)
    down = passed_along(down, 0, -1)
    coords, rest = pl.pallas_call(
        arrive_kernel,
        out_shape=(planes(6), planes(4)),
        in_specs=[SM] + [VM] * 5,
        out_specs=(VM, VM),
        scratch_shapes=[pltpu.VMEM((10, CAPACITY + 8, BLOCK), jnp.float32)],
        compiler_params=PARAMS,
        name="arrive",
    )(staying, stay, left, right, up, down)
    east = passed_along(coords, -1, 0)
    north = passed_along(coords, 0, -1)
    far = sent(coords, -1, -1, 0)
    near = sent(north, -1, 0, 1)
    on_home, on_east, on_north, on_corner = pl.pallas_call(
        pair_kernel,
        out_shape=(planes(3),) * 4,
        in_specs=[SM] + [VM] * 5,
        out_specs=(VM,) * 4,
        scratch_shapes=[pltpu.VMEM((6,4 * CAPACITY,128),jnp.float32)]+[pltpu.VMEM((4 * CAPACITY*8,128),jnp.float32)]*3+[pltpu.VMEM((6,16,8,128),jnp.float32)]*2+[pltpu.VMEM((3,2,16,8,128),jnp.float32)]*2+[pltpu.VMEM((17,8,128),jnp.float32)],
        compiler_params=PARAMS,
        name="pair",
    )(tiles.reshape(18, 128, 2).transpose(0, 2, 1).reshape(-1), coords, east, north, near, far)
    from_near = sent(on_corner, 1, 0, 0)
    from_far = sent(on_corner, 1, 1, 1)
    from_east = passed_along(on_east, 1, 0)
    from_north = passed_along(on_north + from_near, 0, 1)
    out = pl.pallas_call(
        update_kernel,
        out_shape=(planes(3),) * 3,
        in_specs=[VM] * 6,
        out_specs=(VM,) * 3,
        compiler_params=PARAMS,
        name="update",
    )(on_home, from_east, from_north, from_far, coords, rest)
    return tuple(value.reshape(3, 1, 1, CAPACITY * BLOCK) for value in out)


def solution(mesh):
    vector = P(None, "gx", "gy", None)
    scalar = P("gx", "gy", None)
    return jax.shard_map(
        body,
        mesh=mesh,
        in_specs=(vector, vector) + (scalar,) * 5 + (P("gx", "gy", None, None),),
        out_specs=(vector,) * 3,
        check_vma=False,
    )
```

```python
import functools

import jax
import jax.numpy as jnp
from jax import lax
from jax.experimental import pallas as pl
from jax.experimental.pallas import tpu as pltpu
from jax.sharding import PartitionSpec as P

BLOCK = 128
NB = 128
CAPACITY = 144
CELL = 2.0
TSTEP = 0.05
OFFSETS = ((0, 0), (1, 0), (-1, 0), (0, 1), (0, -1), (1, 1), (1, -1), (-1, 1), (-1, -1))
LOG2E = 1.4426950408889634
HALFC = 1.1283791670955126


def passed_along(value, step_x, step_y):
    nx, ny = lax.axis_size("gx"), lax.axis_size("gy")
    if step_y == 0:
        return lax.ppermute(value, "gx", [(s, (s + step_x) % nx) for s in range(nx)])
    if step_x == 0:
        return lax.ppermute(value, "gy", [(s, (s + step_y) % ny) for s in range(ny)])
    pairs = [
        (i * ny + j, ((i + step_x) % nx) * ny + (j + step_y) % ny)
        for i in range(nx)
        for j in range(ny)
    ]
    return lax.ppermute(value, ("gx", "gy"), pairs)


PLACE = (8, 0, 3, 6, 7, 1, 2, 4, 5)


def sent(value, step_x, step_y, parity):
    nx, ny = lax.axis_size("gx"), lax.axis_size("gy")
    if step_y == 0:
        return lax.ppermute(value, "gx", [(s, (s + step_x) % nx) for s in range(nx) if s % 2 == parity])
    pairs = [
        (i * ny + j, ((i + step_x) % nx) * ny + (j + step_y) % ny)
        for i in range(nx)
        for j in range(ny)
        if i % 2 == parity
    ]
    return lax.ppermute(value, ("gx", "gy"), pairs)


def fetch(sources, scratch, arrival):
    copies = [
        pltpu.make_async_copy(source, held, arrival.at[k])
        for k, (source, held) in enumerate(zip(sources, scratch))
    ]
    for copy in copies:
        copy.start()
    return copies


def block_rows(scratch, k):
    pos, vel, chg, rep, dis, inv = scratch[1:7]
    at = pl.ds(k, 1)
    return [pos[d, at, :] for d in range(3)] + [vel[d, at, :] for d in range(3)] + [
        ref[at, :] for ref in (chg, rep, dis, inv)
    ]


def pack_kernel(*refs):
    sources, outs, scratch, tally, arrival = refs[:7], refs[7:10], refs[10:17], refs[17], refs[18]
    parcels = refs[19]
    move = scratch[0]
    copies = fetch(sources, scratch, arrival)
    zero = jnp.zeros((8, BLOCK), jnp.float32)
    for p in range(8):
        for u in range(3):
            parcels[p, 8 * u : 8 * u + 8, :] = zero
    for code in range(9):
        tally[code] = 0
    for copy in copies:
        copy.wait()

    def one(k, carry):
        code = move[k]

        @pl.when(code != 0)
        def _():
            seen = tally[code]
            tally[code] = seen + 1
            to = tally[9 + code]
            slot = jnp.minimum(seen, 1) * 10
            for f, value in enumerate(block_rows(scratch, k)):
                parcels[to, pl.ds(slot + f, 1), :] = value

        return carry

    for code in range(1, 9):
        tally[9 + code] = PLACE[code]
    lax.fori_loop(0, NB, one, 0, unroll=4)
    for code in range(1, 9):
        step_x, step_y = OFFSETS[code]
        to = PLACE[code]
        for n in range(2):
            if step_x != 0:
                parcels[to, 10 * n : 10 * n + 1, :] = parcels[to, 10 * n : 10 * n + 1, :] - step_x * CELL
            if step_y != 0:
                parcels[to, 10 * n + 1 : 10 * n + 2, :] = parcels[to, 10 * n + 1 : 10 * n + 2, :] - step_y * CELL
        parcels[to, 20:21, :] = jnp.broadcast_to(tally[code], (1, BLOCK)).astype(jnp.float32)
    for ref, first in zip(outs, (0, 3, 6)):
        for p in range(ref.shape[0]):
            ref[p] = parcels[first + p]


def stay_kernel(*refs):
    sources, (stay, staying), scratch, arrival = refs[:7], refs[7:9], refs[9:16], refs[16]
    move = scratch[0]
    copies = fetch(sources, scratch, arrival)
    zero = jnp.zeros((8, BLOCK), jnp.float32)
    for f in range(10):
        for u in range(CAPACITY // 8):
            stay[f, 8 * u : 8 * u + 8, :] = zero
    for copy in copies:
        copy.wait()

    def one(k, kept):
        for f, value in enumerate(block_rows(scratch, k)):
            stay[f, pl.ds(kept, 1), :] = value
        return kept + jnp.where(move[k] == 0, 1, 0)

    kept = lax.fori_loop(0, NB, one, 0)
    for f in range(10):
        stay[f, pl.ds(kept, 1), :] = zero[0:1]
    staying[0] = kept


def turn_kernel(staying, own, left, right, up, down):
    up[0], down[0] = own[0], own[1]
    up[1], down[1] = left[1], left[2]
    up[2], down[2] = right[1], right[2]


def arrive_kernel(staying, stay, *refs):
    left, right, up, down, coords, rest, held = refs
    parcels = [left.at[0], right.at[0], up.at[0], down.at[0], up.at[1], down.at[1], up.at[2], down.at[2]]
    for f in range(10):
        held[f, 0:CAPACITY, :] = stay[f]
    counts = jnp.concatenate([p[20:21, :] for p in parcels], axis=0).astype(jnp.int32)
    at = staying[0]
    for code in range(8):
        count = counts[code, 0]
        for n in range(2):
            for f in range(10):
                held[f, pl.ds(at, 1), :] = parcels[code][10 * n + f : 10 * n + f + 1, :]
            at = at + jnp.where(count > n, 1, 0)
    for f in range(10):
        held[f, pl.ds(at, 1), :] = jnp.zeros((1, BLOCK), jnp.float32)
    for k, f in enumerate((0, 1, 2, 6, 7, 8)):
        coords[k] = held[f, 0:CAPACITY, :]
    for k, f in enumerate((3, 4, 5, 9)):
        rest[k] = held[f, 0:CAPACITY, :]


def update_kernel(home, on_i, east, north, coords, rest, new_x, new_v, total):
    for d in range(3):
        force = home[d] + on_i[d] + east[d] + north[d]
        fresh = rest[d] + TSTEP * rest[3] * force
        total[d] = force
        new_v[d] = fresh
        new_x[d] = coords[d] + TSTEP * fresh


def listed(b):
    return (b // 8) * 256 + (b % 8) * 16


def pair_kernel(tiles, home, east, north, near, far, fh, fe, fn, fc, ti, zone, ac0, ac1, ac2, ibuf0, ibuf1, ring, gone, wbuf, *, T=2, mxu=True):
    acc=(ac0,ac1,ac2)
    sub = lax.broadcasted_iota(jnp.int32,(8,128),0)
    lane = lax.broadcasted_iota(jnp.int32,(8,128),1)
    rel = lane//4 - sub//4
    for c in range(16):
        wbuf[c]=jnp.where(rel==2*c,0.0,4.0)
    wbuf[16]=jnp.full((8,128),4.0,jnp.float32)
    for z,(ref,sx,sy) in enumerate(((home,0.,0.),(east,2.,0.),(north,0.,2.),(near,2.,2.))):
        for f in range(6):
            v = ref[f]+far[f] if z==3 else ref[f]
            if f==0 and sx: v=v+sx
            if f==1 and sy: v=v+sy
            if f<3: v=v*2.0
            zone[f, pl.ds(z*CAPACITY,CAPACITY), :] = v
    zero = jnp.zeros((8,128),jnp.float32)
    def clear(k,_):
        for u in range(16):
            for d in range(3):
                acc[d][pl.ds(pl.multiple_of(k*128,128)+8*u,8),:]=zero
        return 0
    lax.fori_loop(0,(4*CAPACITY)//16,clear,0)

    def row(f,j):
        return jnp.broadcast_to(zone[f, pl.ds(j,1), :],(8,128))
    SC=jnp.where(sub==4,6144.0,jnp.where(sub==5,48.0,jnp.where(sub==3,0.25,2.0))).astype(jnp.float32)
    kk=lax.broadcasted_iota(jnp.int32,(24,768),0); nn=lax.broadcasted_iota(jnp.int32,(24,768),1)
    pick=jnp.where(kk%8==nn//128,1.0,0.0).astype(jnp.bfloat16)

    def spread(b,ibuf):
        feat = jnp.concatenate([home[f, pl.ds(b,1), :] for f in range(6)]+[jnp.zeros((2,128),jnp.float32)],axis=0)*SC
        hi=feat.astype(jnp.bfloat16).astype(jnp.float32); r=feat-hi
        mid=r.astype(jnp.bfloat16).astype(jnp.float32); lo=r-mid
        ft=jnp.concatenate([hi,mid,lo],axis=0).T.astype(jnp.bfloat16)
        out=jnp.dot(ft,pick,preferred_element_type=jnp.float32)
        for f in range(6):
            for c in range(16): ibuf[f,c]=out[8*c:8*c+8,128*f:128*f+128]

    def block(b,ibuf,slot,n):
        for c in range(16):
            xi,yi,zi,qi,ai,bi=[ibuf[f,c] for f in range(6)]
            tot=None
            for t in range(T):
                j=tiles[listed(b) + (128 * t + c)]
                dx=xi-row(0,j); dy=yi-row(1,j); dz=zi-row(2,j)
                r2=dx*dx+dy*dy+dz*dz
                w=jnp.maximum(wbuf[jnp.where(j==b,c,16)]-r2,0.0)
                s=jnp.clip(r2,1.0,4.0)
                rs=lax.rsqrt(s)
                inv=rs*rs
                cube=inv*inv*inv
                ew=jnp.exp2(s*-LOG2E)
                kc=(1.0-lax.erf(s*rs))*rs+ew*HALFC
                g=(qi*row(3,j))*kc+cube*((ai*row(4,j))*cube-bi*row(5,j))
                g=g*(inv*(w*w))
                v=(g*dx,g*dy,g*dz)
                j8=pl.ds(pl.multiple_of(j*8,8),8)
                old=[acc[d][j8,:] for d in range(3)]
                for d in range(3):
                    acc[d][j8,:]=old[d]+v[d]
                tot=v if tot is None else tuple(p+q for p,q in zip(tot,v))
            for d in range(3): ring[slot,3*n+d,c]=tot[d]

    RING=3
    spread(0,ibuf0); spread(1,ibuf1)
    def out_copy(k):
        slot=lax.rem(k,RING)
        return pltpu.make_async_copy(ring.at[slot],ti.at[pl.ds(6*k,6)],gone.at[slot])
    def two(k,_):
        b=2*k
        slot=lax.rem(k,RING)
        @pl.when(k>=RING)
        def _(): out_copy(k-RING).wait()
        block(b,ibuf0,slot,0)
        block(b+1,ibuf1,slot,1)
        spread(jnp.minimum(b+2,CAPACITY-1),ibuf0)
        spread(jnp.minimum(b+3,CAPACITY-1),ibuf1)
        out_copy(k).start()
        return 0
    lax.fori_loop(0,CAPACITY//2,two,0)
    def fold(k,_):
        for d in range(3):
            for z,ref in enumerate((fh,fe,fn,fc)):
                k8=pl.multiple_of(k*8,8)
                r=[acc[d][pl.ds((z*CAPACITY+k8)*8+q,8,stride=8),:] for q in range(8)]
                r=((r[0]+r[1])+(r[2]+r[3]))+((r[4]+r[5])+(r[6]+r[7]))
                ref[d,pl.ds(k8,8),:]=-r
        return 0
    lax.fori_loop(0,CAPACITY//8,fold,0)
    for k in range(CAPACITY//2-RING,CAPACITY//2):
        out_copy(k).wait()

def ireduce_kernel(ti,fi):
    lane = lax.broadcasted_iota(jnp.int32,(8,128),1)
    for b in range(8):
        cc=[]
        for c in range(16):
            r=[jnp.sum(ti[3*b+d,c],axis=1,keepdims=True) for d in range(3)]
            cc.append(jnp.where(lane==0,r[0],jnp.where(lane==1,r[1],r[2])))
        m=jnp.concatenate(cc,axis=0)[:, :8].T
        for d in range(3): fi[d,b:b+1,:]=m[d:d+1]


VM = pl.BlockSpec(memory_space=pltpu.VMEM)
SM = pl.BlockSpec(memory_space=pltpu.SMEM)
HBM = pl.BlockSpec(memory_space=pltpu.HBM)
PARAMS = pltpu.CompilerParams(vmem_limit_bytes=48 * 1024 * 1024)
WIDE = pltpu.CompilerParams(vmem_limit_bytes=56 * 1024 * 1024)


def planes(count, rows=CAPACITY):
    return jax.ShapeDtypeStruct((count, rows, BLOCK), jnp.float32)


def body(positions, velocities, charges, repel_root, disperse_root, inverse_mass, move, tiles):
    inputs = (
        move.reshape(NB),
        positions.reshape(3, NB, BLOCK),
        velocities.reshape(3, NB, BLOCK),
        charges.reshape(NB, BLOCK),
        repel_root.reshape(NB, BLOCK),
        disperse_root.reshape(NB, BLOCK),
        inverse_mass.reshape(NB, BLOCK),
    )
    held = (
        [pltpu.SMEM((NB,), jnp.int32)]
        + [pltpu.VMEM((3, NB, BLOCK), jnp.float32)] * 2
        + [pltpu.VMEM((NB, BLOCK), jnp.float32)] * 4
    )
    going_up_x, going_down_x, own = pl.pallas_call(
        pack_kernel,
        out_shape=(planes(3, 24), planes(3, 24), planes(2, 24)),
        in_specs=[HBM] * 7,
        out_specs=(VM,) * 3,
        scratch_shapes=held
        + [pltpu.SMEM((18,), jnp.int32), pltpu.SemaphoreType.DMA((7,)), pltpu.VMEM((8, 24, BLOCK), jnp.float32)],
        compiler_params=WIDE,
        name="pack",
    )(*inputs)
    left = passed_along(going_up_x, 1, 0)
    right = passed_along(going_down_x, -1, 0)
    stay, staying = pl.pallas_call(
        stay_kernel,
        out_shape=(planes(10), jax.ShapeDtypeStruct((1,), jnp.int32)),
        in_specs=[HBM] * 7,
        out_specs=(VM, SM),
        scratch_shapes=held + [pltpu.SemaphoreType.DMA((7,))],
        compiler_params=WIDE,
        cost_estimate=pl.CostEstimate(flops=0, bytes_accessed=6_000_000, transcendentals=0),
        name="stay",
    )(*inputs)
    up, down = pl.pallas_call(
        turn_kernel,
        out_shape=(planes(3, 24),) * 2,
        in_specs=[SM] + [VM] * 3,
        out_specs=(VM,) * 2,
        compiler_params=PARAMS,
        name="turn",
    )(staying, own, left, right)
    up = passed_along(up, 0, 1)
    down = passed_along(down, 0, -1)
    coords, rest = pl.pallas_call(
        arrive_kernel,
        out_shape=(planes(6), planes(4)),
        in_specs=[SM] + [VM] * 5,
        out_specs=(VM, VM),
        scratch_shapes=[pltpu.VMEM((10, CAPACITY + 8, BLOCK), jnp.float32)],
        compiler_params=PARAMS,
        name="arrive",
    )(staying, stay, left, right, up, down)
    east = passed_along(coords, -1, 0)
    north = passed_along(coords, 0, -1)
    far = sent(coords, -1, -1, 0)
    near = sent(north, -1, 0, 1)
    on_home, on_east, on_north, on_corner, sums = pl.pallas_call(
        pair_kernel,
        out_shape=(planes(3),) * 4 + (jax.ShapeDtypeStruct((3 * CAPACITY, 16, 8, BLOCK), jnp.float32),),
        in_specs=[SM] + [VM] * 5,
        out_specs=(VM,) * 4 + (HBM,),
        scratch_shapes=[pltpu.VMEM((6,4 * CAPACITY,128),jnp.float32)]+[pltpu.VMEM((4 * CAPACITY*8,128),jnp.float32)]*3+[pltpu.VMEM((6,16,8,128),jnp.float32)]*2+[pltpu.VMEM((3,6,16,8,128),jnp.float32),pltpu.SemaphoreType.DMA((3,))]+[pltpu.VMEM((17,8,128),jnp.float32)],
        compiler_params=PARAMS,
        name="pair",
    )(tiles.reshape(18, 128, 2).transpose(0, 2, 1).reshape(-1), coords, east, north, near, far)
    from_corner = passed_along(on_corner, 1, 0)
    from_east = passed_along(on_east, 1, 0)
    from_north = passed_along(on_north + from_corner, 0, 1)
    on_i = pl.pallas_call(
        ireduce_kernel,
        grid=(CAPACITY // 8,),
        out_shape=planes(3),
        in_specs=[pl.BlockSpec((24, 16, 8, BLOCK), lambda i: (i, 0, 0, 0))],
        out_specs=pl.BlockSpec((3, 8, BLOCK), lambda i: (0, i, 0)),
        compiler_params=PARAMS,
        cost_estimate=pl.CostEstimate(flops=20_000_000, bytes_accessed=28_000_000, transcendentals=0),
        name="ireduce",
    )(sums)
    out = pl.pallas_call(
        update_kernel,
        out_shape=(planes(3),) * 3,
        in_specs=[VM] * 6,
        out_specs=(VM,) * 3,
        compiler_params=PARAMS,
        name="update",
    )(on_home, on_i, from_east, from_north, coords, rest)
    return tuple(value.reshape(3, 1, 1, CAPACITY * BLOCK) for value in out)


def solution(mesh):
    vector = P(None, "gx", "gy", None)
    scalar = P("gx", "gy", None)
    return jax.shard_map(
        body,
        mesh=mesh,
        in_specs=(vector, vector) + (scalar,) * 5 + (P("gx", "gy", None, None),),
        out_specs=(vector,) * 3,
        check_vma=False,
    )
```

```python
import functools

import jax
import jax.numpy as jnp
from jax import lax
from jax.experimental import pallas as pl
from jax.experimental.pallas import tpu as pltpu
from jax.sharding import PartitionSpec as P

BLOCK = 128
NB = 128
CAPACITY = 144
CELL = 2.0
TSTEP = 0.05
OFFSETS = ((0, 0), (1, 0), (-1, 0), (0, 1), (0, -1), (1, 1), (1, -1), (-1, 1), (-1, -1))
LOG2E = 1.4426950408889634
HALFC = 1.1283791670955126


def passed_along(value, step_x, step_y):
    nx, ny = lax.axis_size("gx"), lax.axis_size("gy")
    if step_y == 0:
        return lax.ppermute(value, "gx", [(s, (s + step_x) % nx) for s in range(nx)])
    if step_x == 0:
        return lax.ppermute(value, "gy", [(s, (s + step_y) % ny) for s in range(ny)])
    pairs = [
        (i * ny + j, ((i + step_x) % nx) * ny + (j + step_y) % ny)
        for i in range(nx)
        for j in range(ny)
    ]
    return lax.ppermute(value, ("gx", "gy"), pairs)


PLACE = (8, 0, 3, 6, 7, 1, 2, 4, 5)


def sent(value, step_x, step_y, parity):
    nx, ny = lax.axis_size("gx"), lax.axis_size("gy")
    if step_y == 0:
        return lax.ppermute(value, "gx", [(s, (s + step_x) % nx) for s in range(nx) if s % 2 == parity])
    pairs = [
        (i * ny + j, ((i + step_x) % nx) * ny + (j + step_y) % ny)
        for i in range(nx)
        for j in range(ny)
        if i % 2 == parity
    ]
    return lax.ppermute(value, ("gx", "gy"), pairs)


def fetch(sources, scratch, arrival):
    copies = [
        pltpu.make_async_copy(source, held, arrival.at[k])
        for k, (source, held) in enumerate(zip(sources, scratch))
    ]
    for copy in copies:
        copy.start()
    return copies


def block_rows(scratch, k):
    pos, vel, chg, rep, dis, inv = scratch[1:7]
    at = pl.ds(k, 1)
    return [pos[d, at, :] for d in range(3)] + [vel[d, at, :] for d in range(3)] + [
        ref[at, :] for ref in (chg, rep, dis, inv)
    ]


def pack_kernel(*refs):
    sources, outs, scratch, tally, arrival = refs[:7], refs[7:10], refs[10:17], refs[17], refs[18]
    parcels = refs[19]
    move = scratch[0]
    copies = fetch(sources, scratch, arrival)
    zero = jnp.zeros((8, BLOCK), jnp.float32)
    for p in range(8):
        for u in range(3):
            parcels[p, 8 * u : 8 * u + 8, :] = zero
    for code in range(9):
        tally[code] = 0
    for copy in copies:
        copy.wait()

    def one(k, carry):
        code = move[k]

        @pl.when(code != 0)
        def _():
            seen = tally[code]
            tally[code] = seen + 1
            to = tally[9 + code]
            slot = jnp.minimum(seen, 1) * 10
            for f, value in enumerate(block_rows(scratch, k)):
                parcels[to, pl.ds(slot + f, 1), :] = value

        return carry

    for code in range(1, 9):
        tally[9 + code] = PLACE[code]
    lax.fori_loop(0, NB, one, 0, unroll=4)
    for code in range(1, 9):
        step_x, step_y = OFFSETS[code]
        to = PLACE[code]
        for n in range(2):
            if step_x != 0:
                parcels[to, 10 * n : 10 * n + 1, :] = parcels[to, 10 * n : 10 * n + 1, :] - step_x * CELL
            if step_y != 0:
                parcels[to, 10 * n + 1 : 10 * n + 2, :] = parcels[to, 10 * n + 1 : 10 * n + 2, :] - step_y * CELL
        parcels[to, 20:21, :] = jnp.broadcast_to(tally[code], (1, BLOCK)).astype(jnp.float32)
    for ref, first in zip(outs, (0, 3, 6)):
        for p in range(ref.shape[0]):
            ref[p] = parcels[first + p]


def stay_kernel(*refs):
    sources, (stay, staying), scratch, arrival = refs[:7], refs[7:9], refs[9:16], refs[16]
    move = scratch[0]
    copies = fetch(sources, scratch, arrival)
    zero = jnp.zeros((8, BLOCK), jnp.float32)
    for f in range(10):
        for u in range(CAPACITY // 8):
            stay[f, 8 * u : 8 * u + 8, :] = zero
    for copy in copies:
        copy.wait()

    def one(k, kept):
        for f, value in enumerate(block_rows(scratch, k)):
            stay[f, pl.ds(kept, 1), :] = value
        return kept + jnp.where(move[k] == 0, 1, 0)

    kept = lax.fori_loop(0, NB, one, 0)
    for f in range(10):
        stay[f, pl.ds(kept, 1), :] = zero[0:1]
    staying[0] = kept


def turn_kernel(staying, own, left, right, up, down):
    up[0], down[0] = own[0], own[1]
    up[1], down[1] = left[1], left[2]
    up[2], down[2] = right[1], right[2]


def arrive_kernel(staying, stay, *refs):
    left, right, up, down, coords, rest, held = refs
    parcels = [left.at[0], right.at[0], up.at[0], down.at[0], up.at[1], down.at[1], up.at[2], down.at[2]]
    for f in range(10):
        held[f, 0:CAPACITY, :] = stay[f]
    counts = jnp.concatenate([p[20:21, :] for p in parcels], axis=0).astype(jnp.int32)
    at = staying[0]
    for code in range(8):
        count = counts[code, 0]
        for n in range(2):
            for f in range(10):
                held[f, pl.ds(at, 1), :] = parcels[code][10 * n + f : 10 * n + f + 1, :]
            at = at + jnp.where(count > n, 1, 0)
    for f in range(10):
        held[f, pl.ds(at, 1), :] = jnp.zeros((1, BLOCK), jnp.float32)
    for k, f in enumerate((0, 1, 2, 6, 7, 8)):
        coords[k] = held[f, 0:CAPACITY, :]
    for k, f in enumerate((3, 4, 5, 9)):
        rest[k] = held[f, 0:CAPACITY, :]


def update_kernel(home, first, second, east, north, coords, rest, new_x, new_v, total):
    for d in range(3):
        on_i = jnp.concatenate([first[d], second[d]], axis=0)
        force = home[d] + on_i + east[d] + north[d]
        fresh = rest[d] + TSTEP * rest[3] * force
        total[d] = force
        new_v[d] = fresh
        new_x[d] = coords[d] + TSTEP * fresh


def listed(b):
    return (b // 8) * 256 + (b % 8) * 16


def pair_kernel(tiles, home, east, north, near, far, fh, fe, fn, fc, ti, zone, ac0, ac1, ac2, ibuf0, ibuf1, ring, gone, wbuf, *, T=2, mxu=True):
    acc=(ac0,ac1,ac2)
    sub = lax.broadcasted_iota(jnp.int32,(8,128),0)
    lane = lax.broadcasted_iota(jnp.int32,(8,128),1)
    rel = lane//4 - sub//4
    for c in range(16):
        wbuf[c]=jnp.where(rel==2*c,0.0,4.0)
    wbuf[16]=jnp.full((8,128),4.0,jnp.float32)
    for z,(ref,sx,sy) in enumerate(((home,0.,0.),(east,2.,0.),(north,0.,2.),(near,2.,2.))):
        for f in range(6):
            v = ref[f]+far[f] if z==3 else ref[f]
            if f==0 and sx: v=v+sx
            if f==1 and sy: v=v+sy
            if f<3: v=v*2.0
            zone[f, pl.ds(z*CAPACITY,CAPACITY), :] = v
    zero = jnp.zeros((8,128),jnp.float32)
    def clear(k,_):
        for u in range(16):
            for d in range(3):
                acc[d][pl.ds(pl.multiple_of(k*128,128)+8*u,8),:]=zero
        return 0
    lax.fori_loop(0,(4*CAPACITY)//16,clear,0)

    def row(f,j):
        return jnp.broadcast_to(zone[f, pl.ds(j,1), :],(8,128))
    SC=jnp.where(sub==4,6144.0,jnp.where(sub==5,48.0,jnp.where(sub==3,0.25,2.0))).astype(jnp.float32)
    kk=lax.broadcasted_iota(jnp.int32,(24,768),0); nn=lax.broadcasted_iota(jnp.int32,(24,768),1)
    pick=jnp.where(kk%8==nn//128,1.0,0.0).astype(jnp.bfloat16)

    def spread(b,ibuf):
        feat = jnp.concatenate([home[f, pl.ds(b,1), :] for f in range(6)]+[jnp.zeros((2,128),jnp.float32)],axis=0)*SC
        hi=feat.astype(jnp.bfloat16).astype(jnp.float32); r=feat-hi
        mid=r.astype(jnp.bfloat16).astype(jnp.float32); lo=r-mid
        ft=jnp.concatenate([hi,mid,lo],axis=0).T.astype(jnp.bfloat16)
        out=jnp.dot(ft,pick,preferred_element_type=jnp.float32)
        for f in range(6):
            for c in range(16): ibuf[f,c]=out[8*c:8*c+8,128*f:128*f+128]

    def block(b,ibuf,slot,n):
        for c in range(16):
            xi,yi,zi,qi,ai,bi=[ibuf[f,c] for f in range(6)]
            tot=None
            for t in range(T):
                j=tiles[listed(b) + (128 * t + c)]
                dx=xi-row(0,j); dy=yi-row(1,j); dz=zi-row(2,j)
                r2=dx*dx+dy*dy+dz*dz
                w=jnp.maximum(wbuf[jnp.where(j==b,c,16)]-r2,0.0)
                s=jnp.clip(r2,1.0,4.0)
                rs=lax.rsqrt(s)
                inv=rs*rs
                cube=inv*inv*inv
                ew=jnp.exp2(s*-LOG2E)
                kc=(1.0-lax.erf(s*rs))*rs+ew*HALFC
                g=(qi*row(3,j))*kc+cube*((ai*row(4,j))*cube-bi*row(5,j))
                g=g*(inv*(w*w))
                v=(g*dx,g*dy,g*dz)
                j8=pl.ds(pl.multiple_of(j*8,8),8)
                old=[acc[d][j8,:] for d in range(3)]
                for d in range(3):
                    acc[d][j8,:]=old[d]+v[d]
                tot=v if tot is None else tuple(p+q for p,q in zip(tot,v))
            for d in range(3): ring[slot,3*n+d,c]=tot[d]

    RING=3
    spread(0,ibuf0); spread(1,ibuf1)
    def out_copy(k):
        slot=lax.rem(k,RING)
        return pltpu.make_async_copy(ring.at[slot],ti.at[pl.ds(6*k,6)],gone.at[slot])
    def two(k,_):
        b=2*k
        slot=lax.rem(k,RING)
        @pl.when(k>=RING)
        def _(): out_copy(k-RING).wait()
        block(b,ibuf0,slot,0)
        block(b+1,ibuf1,slot,1)
        spread(jnp.minimum(b+2,CAPACITY-1),ibuf0)
        spread(jnp.minimum(b+3,CAPACITY-1),ibuf1)
        out_copy(k).start()
        return 0
    lax.fori_loop(0,CAPACITY//2,two,0)
    def fold(k,_):
        for d in range(3):
            for z,ref in enumerate((fh,fe,fn,fc)):
                k8=pl.multiple_of(k*8,8)
                r=[acc[d][pl.ds((z*CAPACITY+k8)*8+q,8,stride=8),:] for q in range(8)]
                r=((r[0]+r[1])+(r[2]+r[3]))+((r[4]+r[5])+(r[6]+r[7]))
                ref[d,pl.ds(k8,8),:]=-r
        return 0
    lax.fori_loop(0,CAPACITY//8,fold,0)
    for k in range(CAPACITY//2-RING,CAPACITY//2):
        out_copy(k).wait()

def ireduce_kernel(*refs):
    fi = refs[8]
    lane = lax.broadcasted_iota(jnp.int32, (8, BLOCK), 1)
    for b in range(8):
        ti = refs[b]
        cc = []
        for c in range(16):
            r = [jnp.sum(ti[d, c], axis=1, keepdims=True) for d in range(3)]
            cc.append(jnp.where(lane == 0, r[0], jnp.where(lane == 1, r[1], r[2])))
        m = jnp.concatenate(cc, axis=0)[:, :8].T
        for d in range(3):
            fi[d, b : b + 1, :] = m[d : d + 1]


def onward_kernel(first, on_north, from_corner, out):
    for d in range(3):
        out[d] = on_north[d] + from_corner[d]


VM = pl.BlockSpec(memory_space=pltpu.VMEM)
SM = pl.BlockSpec(memory_space=pltpu.SMEM)
HBM = pl.BlockSpec(memory_space=pltpu.HBM)
PARAMS = pltpu.CompilerParams(vmem_limit_bytes=48 * 1024 * 1024)
WIDE = pltpu.CompilerParams(vmem_limit_bytes=56 * 1024 * 1024)


def planes(count, rows=CAPACITY):
    return jax.ShapeDtypeStruct((count, rows, BLOCK), jnp.float32)


def lane_sums(sums, step):
    def stream(n):
        return pl.BlockSpec((3, 16, 8, BLOCK), lambda i: (8 * (i + step) + n, 0, 0, 0))

    return pl.pallas_call(
        ireduce_kernel,
        grid=(CAPACITY // 16,),
        out_shape=planes(3, CAPACITY // 2),
        in_specs=[stream(n) for n in range(8)],
        out_specs=pl.BlockSpec((3, 8, BLOCK), lambda i: (0, i, 0)),
        compiler_params=PARAMS,
        cost_estimate=pl.CostEstimate(flops=10_000_000, bytes_accessed=14_000_000, transcendentals=0),
        name="lane_sums",
    )(*[sums] * 8)


def body(positions, velocities, charges, repel_root, disperse_root, inverse_mass, move, tiles):
    inputs = (
        move.reshape(NB),
        positions.reshape(3, NB, BLOCK),
        velocities.reshape(3, NB, BLOCK),
        charges.reshape(NB, BLOCK),
        repel_root.reshape(NB, BLOCK),
        disperse_root.reshape(NB, BLOCK),
        inverse_mass.reshape(NB, BLOCK),
    )
    held = (
        [pltpu.SMEM((NB,), jnp.int32)]
        + [pltpu.VMEM((3, NB, BLOCK), jnp.float32)] * 2
        + [pltpu.VMEM((NB, BLOCK), jnp.float32)] * 4
    )
    going_up_x, going_down_x, own = pl.pallas_call(
        pack_kernel,
        out_shape=(planes(3, 24), planes(3, 24), planes(2, 24)),
        in_specs=[HBM] * 7,
        out_specs=(VM,) * 3,
        scratch_shapes=held
        + [pltpu.SMEM((18,), jnp.int32), pltpu.SemaphoreType.DMA((7,)), pltpu.VMEM((8, 24, BLOCK), jnp.float32)],
        compiler_params=WIDE,
        name="pack",
    )(*inputs)
    left = passed_along(going_up_x, 1, 0)
    right = passed_along(going_down_x, -1, 0)
    stay, staying = pl.pallas_call(
        stay_kernel,
        out_shape=(planes(10), jax.ShapeDtypeStruct((1,), jnp.int32)),
        in_specs=[HBM] * 7,
        out_specs=(VM, SM),
        scratch_shapes=held + [pltpu.SemaphoreType.DMA((7,))],
        compiler_params=WIDE,
        cost_estimate=pl.CostEstimate(flops=0, bytes_accessed=6_000_000, transcendentals=0),
        name="stay",
    )(*inputs)
    up, down = pl.pallas_call(
        turn_kernel,
        out_shape=(planes(3, 24),) * 2,
        in_specs=[SM] + [VM] * 3,
        out_specs=(VM,) * 2,
        compiler_params=PARAMS,
        name="turn",
    )(staying, own, left, right)
    up = passed_along(up, 0, 1)
    down = passed_along(down, 0, -1)
    coords, rest = pl.pallas_call(
        arrive_kernel,
        out_shape=(planes(6), planes(4)),
        in_specs=[SM] + [VM] * 5,
        out_specs=(VM, VM),
        scratch_shapes=[pltpu.VMEM((10, CAPACITY + 8, BLOCK), jnp.float32)],
        compiler_params=PARAMS,
        name="arrive",
    )(staying, stay, left, right, up, down)
    east = passed_along(coords, -1, 0)
    north = passed_along(coords, 0, -1)
    far = sent(coords, -1, -1, 0)
    near = sent(north, -1, 0, 1)
    on_home, on_east, on_north, on_corner, sums = pl.pallas_call(
        pair_kernel,
        out_shape=(planes(3),) * 4 + (jax.ShapeDtypeStruct((3 * CAPACITY, 16, 8, BLOCK), jnp.float32),),
        in_specs=[SM] + [VM] * 5,
        out_specs=(VM,) * 4 + (HBM,),
        scratch_shapes=[pltpu.VMEM((6,4 * CAPACITY,128),jnp.float32)]+[pltpu.VMEM((4 * CAPACITY*8,128),jnp.float32)]*3+[pltpu.VMEM((6,16,8,128),jnp.float32)]*2+[pltpu.VMEM((3,6,16,8,128),jnp.float32),pltpu.SemaphoreType.DMA((3,))]+[pltpu.VMEM((17,8,128),jnp.float32)],
        compiler_params=PARAMS,
        name="pair",
    )(tiles.reshape(18, 128, 2).transpose(0, 2, 1).reshape(-1), coords, east, north, near, far)
    from_corner = passed_along(on_corner, 1, 0)
    from_east = passed_along(on_east, 1, 0)
    first = lane_sums(sums, 0)
    onward = pl.pallas_call(
        onward_kernel,
        out_shape=planes(3),
        in_specs=[pl.BlockSpec(memory_space=pl.ANY)] + [VM] * 2,
        out_specs=VM,
        compiler_params=PARAMS,
        name="onward",
    )(first, on_north, from_corner)
    from_north = passed_along(onward, 0, 1)
    second = lane_sums(sums, CAPACITY // 16)
    out = pl.pallas_call(
        update_kernel,
        out_shape=(planes(3),) * 3,
        in_specs=[VM] * 7,
        out_specs=(VM,) * 3,
        compiler_params=PARAMS,
        name="update",
    )(on_home, first, second, from_east, from_north, coords, rest)
    return tuple(value.reshape(3, 1, 1, CAPACITY * BLOCK) for value in out)


def solution(mesh):
    vector = P(None, "gx", "gy", None)
    scalar = P("gx", "gy", None)
    return jax.shard_map(
        body,
        mesh=mesh,
        in_specs=(vector, vector) + (scalar,) * 5 + (P("gx", "gy", None, None),),
        out_specs=(vector,) * 3,
        check_vma=False,
    )
```

```python
import functools

import jax
import jax.numpy as jnp
from jax import lax
from jax.experimental import pallas as pl
from jax.experimental.pallas import tpu as pltpu
from jax.sharding import PartitionSpec as P

BLOCK = 128
NB = 128
CAPACITY = 144
CELL = 2.0
TSTEP = 0.05
OFFSETS = ((0, 0), (1, 0), (-1, 0), (0, 1), (0, -1), (1, 1), (1, -1), (-1, 1), (-1, -1))
LOG2E = 1.4426950408889634
HALFC = 1.1283791670955126


def passed_along(value, step_x, step_y):
    nx, ny = lax.axis_size("gx"), lax.axis_size("gy")
    if step_y == 0:
        return lax.ppermute(value, "gx", [(s, (s + step_x) % nx) for s in range(nx)])
    if step_x == 0:
        return lax.ppermute(value, "gy", [(s, (s + step_y) % ny) for s in range(ny)])
    pairs = [
        (i * ny + j, ((i + step_x) % nx) * ny + (j + step_y) % ny)
        for i in range(nx)
        for j in range(ny)
    ]
    return lax.ppermute(value, ("gx", "gy"), pairs)


PLACE = (8, 0, 3, 6, 7, 1, 2, 4, 5)


def sent(value, step_x, step_y, parity):
    nx, ny = lax.axis_size("gx"), lax.axis_size("gy")
    if step_y == 0:
        return lax.ppermute(value, "gx", [(s, (s + step_x) % nx) for s in range(nx) if s % 2 == parity])
    pairs = [
        (i * ny + j, ((i + step_x) % nx) * ny + (j + step_y) % ny)
        for i in range(nx)
        for j in range(ny)
        if i % 2 == parity
    ]
    return lax.ppermute(value, ("gx", "gy"), pairs)


def fetch(sources, scratch, arrival):
    copies = [
        pltpu.make_async_copy(source, held, arrival.at[k])
        for k, (source, held) in enumerate(zip(sources, scratch))
    ]
    for copy in copies:
        copy.start()
    return copies


def block_rows(scratch, k):
    pos, vel, chg, rep, dis, inv = scratch[1:7]
    at = pl.ds(k, 1)
    return [pos[d, at, :] for d in range(3)] + [vel[d, at, :] for d in range(3)] + [
        ref[at, :] for ref in (chg, rep, dis, inv)
    ]


def pack_kernel(*refs):
    sources, outs, scratch, tally, arrival = refs[:7], refs[7:10], refs[10:17], refs[17], refs[18]
    parcels = refs[19]
    move = scratch[0]
    copies = fetch(sources, scratch, arrival)
    zero = jnp.zeros((8, BLOCK), jnp.float32)
    for p in range(8):
        for u in range(3):
            parcels[p, 8 * u : 8 * u + 8, :] = zero
    for code in range(9):
        tally[code] = 0
    for copy in copies:
        copy.wait()

    def one(k, carry):
        code = move[k]

        @pl.when(code != 0)
        def _():
            seen = tally[code]
            tally[code] = seen + 1
            to = tally[9 + code]
            slot = jnp.minimum(seen, 1) * 10
            for f, value in enumerate(block_rows(scratch, k)):
                parcels[to, pl.ds(slot + f, 1), :] = value

        return carry

    for code in range(1, 9):
        tally[9 + code] = PLACE[code]
    lax.fori_loop(0, NB, one, 0, unroll=4)
    for code in range(1, 9):
        step_x, step_y = OFFSETS[code]
        to = PLACE[code]
        for n in range(2):
            if step_x != 0:
                parcels[to, 10 * n : 10 * n + 1, :] = parcels[to, 10 * n : 10 * n + 1, :] - step_x * CELL
            if step_y != 0:
                parcels[to, 10 * n + 1 : 10 * n + 2, :] = parcels[to, 10 * n + 1 : 10 * n + 2, :] - step_y * CELL
        parcels[to, 20:21, :] = jnp.broadcast_to(tally[code], (1, BLOCK)).astype(jnp.float32)
    for ref, first in zip(outs, (0, 3, 6)):
        for p in range(ref.shape[0]):
            ref[p] = parcels[first + p]


def stay_kernel(*refs):
    sources, (stay, staying), scratch, arrival = refs[:7], refs[7:9], refs[9:16], refs[16]
    move = scratch[0]
    copies = fetch(sources, scratch, arrival)
    zero = jnp.zeros((8, BLOCK), jnp.float32)
    for f in range(10):
        for u in range(CAPACITY // 8):
            stay[f, 8 * u : 8 * u + 8, :] = zero
    for copy in copies:
        copy.wait()

    def one(k, kept):
        for f, value in enumerate(block_rows(scratch, k)):
            stay[f, pl.ds(kept, 1), :] = value
        return kept + jnp.where(move[k] == 0, 1, 0)

    kept = lax.fori_loop(0, NB, one, 0)
    for f in range(10):
        stay[f, pl.ds(kept, 1), :] = zero[0:1]
    staying[0] = kept


def turn_kernel(staying, own, left, right, up, down):
    up[0], down[0] = own[0], own[1]
    up[1], down[1] = left[1], left[2]
    up[2], down[2] = right[1], right[2]


def arrive_kernel(staying, stay, *refs):
    left, right, up, down, coords, rest, held = refs
    parcels = [left.at[0], right.at[0], up.at[0], down.at[0], up.at[1], down.at[1], up.at[2], down.at[2]]
    for f in range(10):
        held[f, 0:CAPACITY, :] = stay[f]
    counts = jnp.concatenate([p[20:21, :] for p in parcels], axis=0).astype(jnp.int32)
    at = staying[0]
    for code in range(8):
        count = counts[code, 0]
        for n in range(2):
            for f in range(10):
                held[f, pl.ds(at, 1), :] = parcels[code][10 * n + f : 10 * n + f + 1, :]
            at = at + jnp.where(count > n, 1, 0)
    for f in range(10):
        held[f, pl.ds(at, 1), :] = jnp.zeros((1, BLOCK), jnp.float32)
    for k, f in enumerate((0, 1, 2, 6, 7, 8)):
        coords[k] = held[f, 0:CAPACITY, :]
    for k, f in enumerate((3, 4, 5, 9)):
        rest[k] = held[f, 0:CAPACITY, :]


def update_kernel(home, east, north, coords, rest, new_x, new_v, total):
    for d in range(3):
        force = home[d] + east[d] + north[d]
        fresh = rest[d] + TSTEP * rest[3] * force
        total[d] = force
        new_v[d] = fresh
        new_x[d] = coords[d] + TSTEP * fresh


def listed(b):
    return (b // 8) * 256 + (b % 8) * 16


def pair_kernel(tiles, home, east, north, near, far, fh, fe, fn, fc, zone, ac0, ac1, ac2, ibuf0, ibuf1, vbuf0, vbuf1, wbuf, *, T=2, mxu=True):
    acc=(ac0,ac1,ac2)
    sub = lax.broadcasted_iota(jnp.int32,(8,128),0)
    lane = lax.broadcasted_iota(jnp.int32,(8,128),1)
    rel = lane//4 - sub//4
    for c in range(16):
        wbuf[c]=jnp.where(rel==2*c,0.0,4.0)
    wbuf[16]=jnp.full((8,128),4.0,jnp.float32)
    for z,(ref,sx,sy) in enumerate(((home,0.,0.),(east,2.,0.),(north,0.,2.),(near,2.,2.))):
        for f in range(6):
            v = ref[f]+far[f] if z==3 else ref[f]
            if f==0 and sx: v=v+sx
            if f==1 and sy: v=v+sy
            if f<3: v=v*2.0
            zone[f, pl.ds(z*CAPACITY,CAPACITY), :] = v
    zero = jnp.zeros((8,128),jnp.float32)
    def clear(k,_):
        for u in range(16):
            for d in range(3):
                acc[d][pl.ds(pl.multiple_of(k*128,128)+8*u,8),:]=zero
        return 0
    lax.fori_loop(0,(4*CAPACITY)//16,clear,0)

    def row(f,j):
        return jnp.broadcast_to(zone[f, pl.ds(j,1), :],(8,128))
    SC=jnp.where(sub==4,6144.0,jnp.where(sub==5,48.0,jnp.where(sub==3,0.25,2.0))).astype(jnp.float32)
    kk=lax.broadcasted_iota(jnp.int32,(24,768),0); nn=lax.broadcasted_iota(jnp.int32,(24,768),1)
    pick=jnp.where(kk%8==nn//128,1.0,0.0).astype(jnp.bfloat16)

    def spread(b,ibuf):
        feat = jnp.concatenate([home[f, pl.ds(b,1), :] for f in range(6)]+[jnp.zeros((2,128),jnp.float32)],axis=0)*SC
        hi=feat.astype(jnp.bfloat16).astype(jnp.float32); r=feat-hi
        mid=r.astype(jnp.bfloat16).astype(jnp.float32); lo=r-mid
        ft=jnp.concatenate([hi,mid,lo],axis=0).T.astype(jnp.bfloat16)
        out=jnp.dot(ft,pick,preferred_element_type=jnp.float32)
        for f in range(6):
            for c in range(16): ibuf[f,c]=out[8*c:8*c+8,128*f:128*f+128]

    def settle(b,vbuf):
        tots=[]
        for c in range(16):
            tot=None
            for t in range(T):
                j8=pl.multiple_of(tiles[listed(b) + (128 * t + c)]*8,8)
                v=[vbuf[d,t,c] for d in range(3)]
                for d in range(3):
                    acc[d][pl.ds(j8,8),:]=acc[d][pl.ds(j8,8),:]+v[d]
                tot=v if tot is None else [p+q for p,q in zip(tot,v)]
            tots.append(tot)
        cc=[]
        for c in range(16):
            r=[jnp.sum(tots[c][d],axis=1,keepdims=True) for d in range(3)]
            cc.append(jnp.where(lane==0,r[0],jnp.where(lane==1,r[1],r[2])))
        m=jnp.concatenate(cc,axis=0)[:, :8].T
        for d in range(3):
            fh[d,pl.ds(b,1),:]=m[d:d+1]

    def block(b,ibuf,vbuf):
        for c in range(16):
            xi,yi,zi,qi,ai,bi=[ibuf[f,c] for f in range(6)]
            for t in range(T):
                j=tiles[listed(b) + (128 * t + c)]
                dx=xi-row(0,j); dy=yi-row(1,j); dz=zi-row(2,j)
                r2=dx*dx+dy*dy+dz*dz
                w=jnp.maximum(wbuf[jnp.where(j==b,c,16)]-r2,0.0)
                s=jnp.clip(r2,1.0,4.0)
                rs=lax.rsqrt(s)
                inv=rs*rs
                cube=inv*inv*inv
                ew=jnp.exp2(s*-LOG2E)
                kc=(1.0-lax.erf(s*rs))*rs+ew*HALFC
                g=(qi*row(3,j))*kc+cube*((ai*row(4,j))*cube-bi*row(5,j))
                g=g*(inv*(w*w))
                vbuf[0,t,c]=g*dx
                vbuf[1,t,c]=g*dy
                vbuf[2,t,c]=g*dz

    spread(0,ibuf0)
    for d in range(3):
        for t in range(T):
            for c in range(16): vbuf1[d,t,c]=zero
    ib=(ibuf0,ibuf0); vb=(vbuf0,vbuf1)
    def some(k,_):
        b=4*k
        for n in range(4):
            settle(jnp.maximum(b+n-1,0),vb[(n+1)%2])
            pass
            block(b+n,ib[n%2],vb[n%2])
            spread(jnp.minimum(b+n+1,CAPACITY-1),ib[(n+1)%2])
        return 0
    lax.fori_loop(0,CAPACITY//4,some,0)
    settle(CAPACITY-1,vb[1])
    for d in range(3):
        for z,ref in enumerate((fh,fe,fn,fc)):
            def red(k,_):
                for u in range(3):
                    k8=pl.multiple_of(k*24+8*u,8)
                    r=[acc[d][pl.ds((z*CAPACITY+k8)*8+q,8,stride=8),:] for q in range(8)]
                    r=((r[0]+r[1])+(r[2]+r[3]))+((r[4]+r[5])+(r[6]+r[7]))
                    if z==0: ref[d,pl.ds(k8,8),:]=ref[d,pl.ds(k8,8),:]-r
                    else: ref[d,pl.ds(k8,8),:]=-r
                return 0
            lax.fori_loop(0,CAPACITY//24,red,0)

VM = pl.BlockSpec(memory_space=pltpu.VMEM)
SM = pl.BlockSpec(memory_space=pltpu.SMEM)
HBM = pl.BlockSpec(memory_space=pltpu.HBM)
PARAMS = pltpu.CompilerParams(vmem_limit_bytes=48 * 1024 * 1024)
WIDE = pltpu.CompilerParams(vmem_limit_bytes=56 * 1024 * 1024)


def planes(count, rows=CAPACITY):
    return jax.ShapeDtypeStruct((count, rows, BLOCK), jnp.float32)


def body(positions, velocities, charges, repel_root, disperse_root, inverse_mass, move, tiles):
    inputs = (
        move.reshape(NB),
        positions.reshape(3, NB, BLOCK),
        velocities.reshape(3, NB, BLOCK),
        charges.reshape(NB, BLOCK),
        repel_root.reshape(NB, BLOCK),
        disperse_root.reshape(NB, BLOCK),
        inverse_mass.reshape(NB, BLOCK),
    )
    held = (
        [pltpu.SMEM((NB,), jnp.int32)]
        + [pltpu.VMEM((3, NB, BLOCK), jnp.float32)] * 2
        + [pltpu.VMEM((NB, BLOCK), jnp.float32)] * 4
    )
    going_up_x, going_down_x, own = pl.pallas_call(
        pack_kernel,
        out_shape=(planes(3, 24), planes(3, 24), planes(2, 24)),
        in_specs=[HBM] * 7,
        out_specs=(VM,) * 3,
        scratch_shapes=held
        + [pltpu.SMEM((18,), jnp.int32), pltpu.SemaphoreType.DMA((7,)), pltpu.VMEM((8, 24, BLOCK), jnp.float32)],
        compiler_params=WIDE,
        name="pack",
    )(*inputs)
    left = passed_along(going_up_x, 1, 0)
    right = passed_along(going_down_x, -1, 0)
    stay, staying = pl.pallas_call(
        stay_kernel,
        out_shape=(planes(10), jax.ShapeDtypeStruct((1,), jnp.int32)),
        in_specs=[HBM] * 7,
        out_specs=(VM, SM),
        scratch_shapes=held + [pltpu.SemaphoreType.DMA((7,))],
        compiler_params=WIDE,
        cost_estimate=pl.CostEstimate(flops=0, bytes_accessed=6_000_000, transcendentals=0),
        name="stay",
    )(*inputs)
    up, down = pl.pallas_call(
        turn_kernel,
        out_shape=(planes(3, 24),) * 2,
        in_specs=[SM] + [VM] * 3,
        out_specs=(VM,) * 2,
        compiler_params=PARAMS,
        name="turn",
    )(staying, own, left, right)
    up = passed_along(up, 0, 1)
    down = passed_along(down, 0, -1)
    coords, rest = pl.pallas_call(
        arrive_kernel,
        out_shape=(planes(6), planes(4)),
        in_specs=[SM] + [VM] * 5,
        out_specs=(VM, VM),
        scratch_shapes=[pltpu.VMEM((10, CAPACITY + 8, BLOCK), jnp.float32)],
        compiler_params=PARAMS,
        name="arrive",
    )(staying, stay, left, right, up, down)
    east = passed_along(coords, -1, 0)
    north = passed_along(coords, 0, -1)
    far = sent(coords, -1, -1, 0)
    near = sent(north, -1, 0, 1)
    on_home, on_east, on_north, on_corner = pl.pallas_call(
        pair_kernel,
        out_shape=(planes(3),) * 4,
        in_specs=[SM] + [VM] * 5,
        out_specs=(VM,) * 4,
        scratch_shapes=[pltpu.VMEM((6,4 * CAPACITY,128),jnp.float32)]+[pltpu.VMEM((4 * CAPACITY*8,128),jnp.float32)]*3+[pltpu.VMEM((6,16,8,128),jnp.float32)]*2+[pltpu.VMEM((3,2,16,8,128),jnp.float32)]*2+[pltpu.VMEM((17,8,128),jnp.float32)],
        compiler_params=PARAMS,
        name="pair",
    )(tiles.reshape(18, 128, 2).transpose(0, 2, 1).reshape(-1), coords, east, north, near, far)
    from_corner = passed_along(on_corner, 1, 0)
    from_east = passed_along(on_east, 1, 0)
    from_north = passed_along(on_north + from_corner, 0, 1)
    out = pl.pallas_call(
        update_kernel,
        out_shape=(planes(3),) * 3,
        in_specs=[VM] * 5,
        out_specs=(VM,) * 3,
        compiler_params=PARAMS,
        name="update",
    )(on_home, from_east, from_north, coords, rest)
    return tuple(value.reshape(3, 1, 1, CAPACITY * BLOCK) for value in out)


def solution(mesh):
    vector = P(None, "gx", "gy", None)
    scalar = P("gx", "gy", None)
    return jax.shard_map(
        body,
        mesh=mesh,
        in_specs=(vector, vector) + (scalar,) * 5 + (P("gx", "gy", None, None),),
        out_specs=(vector,) * 3,
        check_vma=False,
    )
```

```python
import functools

import jax
import jax.numpy as jnp
from jax import lax
from jax.experimental import pallas as pl
from jax.experimental.pallas import tpu as pltpu
from jax.sharding import PartitionSpec as P

BLOCK = 128
NB = 128
CAPACITY = 144
CELL = 2.0
TSTEP = 0.05
OFFSETS = ((0, 0), (1, 0), (-1, 0), (0, 1), (0, -1), (1, 1), (1, -1), (-1, 1), (-1, -1))
LOG2E = 1.4426950408889634
HALFC = 1.1283791670955126


def passed_along(value, step_x, step_y):
    nx, ny = lax.axis_size("gx"), lax.axis_size("gy")
    if step_y == 0:
        return lax.ppermute(value, "gx", [(s, (s + step_x) % nx) for s in range(nx)])
    if step_x == 0:
        return lax.ppermute(value, "gy", [(s, (s + step_y) % ny) for s in range(ny)])
    pairs = [
        (i * ny + j, ((i + step_x) % nx) * ny + (j + step_y) % ny)
        for i in range(nx)
        for j in range(ny)
    ]
    return lax.ppermute(value, ("gx", "gy"), pairs)


PLACE = (8, 0, 3, 6, 7, 1, 2, 4, 5)


def fetch(sources, scratch, arrival):
    copies = [
        pltpu.make_async_copy(source, held, arrival.at[k])
        for k, (source, held) in enumerate(zip(sources, scratch))
    ]
    for copy in copies:
        copy.start()
    return copies


def block_rows(scratch, k):
    pos, vel, chg, rep, dis, inv = scratch[1:7]
    at = pl.ds(k, 1)
    return [pos[d, at, :] for d in range(3)] + [vel[d, at, :] for d in range(3)] + [
        ref[at, :] for ref in (chg, rep, dis, inv)
    ]


def pack_kernel(*refs):
    sources, outs, scratch, tally, arrival = refs[:7], refs[7:10], refs[10:17], refs[17], refs[18]
    parcels = refs[19]
    move = scratch[0]
    copies = fetch(sources, scratch, arrival)
    zero = jnp.zeros((8, BLOCK), jnp.float32)
    for p in range(8):
        for u in range(3):
            parcels[p, 8 * u : 8 * u + 8, :] = zero
    for code in range(9):
        tally[code] = 0
    for copy in copies:
        copy.wait()

    def one(k, carry):
        code = move[k]

        @pl.when(code != 0)
        def _():
            seen = tally[code]
            tally[code] = seen + 1
            to = tally[9 + code]
            slot = jnp.minimum(seen, 1) * 10
            for f, value in enumerate(block_rows(scratch, k)):
                parcels[to, pl.ds(slot + f, 1), :] = value

        return carry

    for code in range(1, 9):
        tally[9 + code] = PLACE[code]
    lax.fori_loop(0, NB, one, 0, unroll=4)
    for code in range(1, 9):
        step_x, step_y = OFFSETS[code]
        to = PLACE[code]
        for n in range(2):
            if step_x != 0:
                parcels[to, 10 * n : 10 * n + 1, :] = parcels[to, 10 * n : 10 * n + 1, :] - step_x * CELL
            if step_y != 0:
                parcels[to, 10 * n + 1 : 10 * n + 2, :] = parcels[to, 10 * n + 1 : 10 * n + 2, :] - step_y * CELL
        parcels[to, 20:21, :] = jnp.broadcast_to(tally[code], (1, BLOCK)).astype(jnp.float32)
    for ref, first in zip(outs, (0, 3, 6)):
        for p in range(ref.shape[0]):
            ref[p] = parcels[first + p]


def stay_kernel(*refs):
    sources, (stay, staying), scratch, arrival = refs[:7], refs[7:9], refs[9:16], refs[16]
    move = scratch[0]
    copies = fetch(sources, scratch, arrival)
    zero = jnp.zeros((8, BLOCK), jnp.float32)
    for f in range(10):
        for u in range(CAPACITY // 8):
            stay[f, 8 * u : 8 * u + 8, :] = zero
    for copy in copies:
        copy.wait()

    def one(k, kept):
        for f, value in enumerate(block_rows(scratch, k)):
            stay[f, pl.ds(kept, 1), :] = value
        return kept + jnp.where(move[k] == 0, 1, 0)

    kept = lax.fori_loop(0, NB, one, 0)
    for f in range(10):
        stay[f, pl.ds(kept, 1), :] = zero[0:1]
    staying[0] = kept


def turn_kernel(staying, own, left, right, up, down):
    up[0], down[0] = own[0], own[1]
    up[1], down[1] = left[1], left[2]
    up[2], down[2] = right[1], right[2]


def arrive_kernel(staying, stay, *refs):
    left, right, up, down, coords, rest, held = refs
    parcels = [left.at[0], right.at[0], up.at[0], down.at[0], up.at[1], down.at[1], up.at[2], down.at[2]]
    for f in range(10):
        held[f, 0:CAPACITY, :] = stay[f]
    counts = jnp.concatenate([p[20:21, :] for p in parcels], axis=0).astype(jnp.int32)
    at = staying[0]
    for code in range(8):
        count = counts[code, 0]
        for n in range(2):
            for f in range(10):
                held[f, pl.ds(at, 1), :] = parcels[code][10 * n + f : 10 * n + f + 1, :]
            at = at + jnp.where(count > n, 1, 0)
    for f in range(10):
        held[f, pl.ds(at, 1), :] = jnp.zeros((1, BLOCK), jnp.float32)
    for k, f in enumerate((0, 1, 2, 6, 7, 8)):
        coords[k] = held[f, 0:CAPACITY, :]
    for k, f in enumerate((3, 4, 5, 9)):
        rest[k] = held[f, 0:CAPACITY, :]


def update_kernel(home, east, north, coords, rest, new_x, new_v, total):
    for d in range(3):
        force = home[d] + east[d] + north[d]
        fresh = rest[d] + TSTEP * rest[3] * force
        total[d] = force
        new_v[d] = fresh
        new_x[d] = coords[d] + TSTEP * fresh


def listed(b):
    return (b // 8) * 256 + (b % 8) * 16


def pair_kernel(tiles, home, east, north, corner, fh, fe, fn, fc, zone, ac0, ac1, ac2, ibuf0, ibuf1, vbuf0, vbuf1, wbuf, *, T=2, mxu=True):
    acc=(ac0,ac1,ac2)
    sub = lax.broadcasted_iota(jnp.int32,(8,128),0)
    lane = lax.broadcasted_iota(jnp.int32,(8,128),1)
    rel = lane//4 - sub//4
    for c in range(16):
        wbuf[c]=jnp.where(rel==2*c,0.0,4.0)
    wbuf[16]=jnp.full((8,128),4.0,jnp.float32)
    for z,(ref,sx,sy) in enumerate(((home,0.,0.),(east,2.,0.),(north,0.,2.),(corner,2.,2.))):
        for f in range(6):
            v = ref[f]
            if f==0 and sx: v=v+sx
            if f==1 and sy: v=v+sy
            if f<3: v=v*2.0
            zone[f, pl.ds(z*CAPACITY,CAPACITY), :] = v
    zero = jnp.zeros((8,128),jnp.float32)
    def clear(k,_):
        for u in range(16):
            for d in range(3):
                acc[d][pl.ds(pl.multiple_of(k*128,128)+8*u,8),:]=zero
        return 0
    lax.fori_loop(0,(4*CAPACITY)//16,clear,0)

    def row(f,j):
        return jnp.broadcast_to(zone[f, pl.ds(j,1), :],(8,128))
    SC=jnp.where(sub==4,6144.0,jnp.where(sub==5,48.0,jnp.where(sub==3,0.25,2.0))).astype(jnp.float32)
    kk=lax.broadcasted_iota(jnp.int32,(24,768),0); nn=lax.broadcasted_iota(jnp.int32,(24,768),1)
    pick=jnp.where(kk%8==nn//128,1.0,0.0).astype(jnp.bfloat16)

    def spread(b,ibuf):
        feat = jnp.concatenate([home[f, pl.ds(b,1), :] for f in range(6)]+[jnp.zeros((2,128),jnp.float32)],axis=0)*SC
        hi=feat.astype(jnp.bfloat16).astype(jnp.float32); r=feat-hi
        mid=r.astype(jnp.bfloat16).astype(jnp.float32); lo=r-mid
        ft=jnp.concatenate([hi,mid,lo],axis=0).T.astype(jnp.bfloat16)
        out=jnp.dot(ft,pick,preferred_element_type=jnp.float32)
        for f in range(6):
            for c in range(16): ibuf[f,c]=out[8*c:8*c+8,128*f:128*f+128]

    def settle(b,vbuf):
        tots=[]
        for c in range(16):
            tot=None
            for t in range(T):
                j8=pl.multiple_of(tiles[listed(b) + (128 * t + c)]*8,8)
                v=[vbuf[d,t,c] for d in range(3)]
                for d in range(3):
                    acc[d][pl.ds(j8,8),:]=acc[d][pl.ds(j8,8),:]+v[d]
                tot=v if tot is None else [p+q for p,q in zip(tot,v)]
            tots.append(tot)
        cc=[]
        for c in range(16):
            r=[jnp.sum(tots[c][d],axis=1,keepdims=True) for d in range(3)]
            cc.append(jnp.where(lane==0,r[0],jnp.where(lane==1,r[1],r[2])))
        m=jnp.concatenate(cc,axis=0)[:, :8].T
        for d in range(3):
            fh[d,pl.ds(b,1),:]=m[d:d+1]

    def block(b,ibuf,vbuf):
        for c in range(16):
            xi,yi,zi,qi,ai,bi=[ibuf[f,c] for f in range(6)]
            for t in range(T):
                j=tiles[listed(b) + (128 * t + c)]
                dx=xi-row(0,j); dy=yi-row(1,j); dz=zi-row(2,j)
                r2=dx*dx+dy*dy+dz*dz
                w=jnp.maximum(wbuf[jnp.where(j==b,c,16)]-r2,0.0)
                s=jnp.clip(r2,1.0,4.0)
                rs=lax.rsqrt(s)
                inv=rs*rs
                cube=inv*inv*inv
                ew=jnp.exp2(s*-LOG2E)
                kc=(1.0-lax.erf(s*rs))*rs+ew*HALFC
                g=(qi*row(3,j))*kc+cube*((ai*row(4,j))*cube-bi*row(5,j))
                g=g*(inv*(w*w))
                vbuf[0,t,c]=g*dx
                vbuf[1,t,c]=g*dy
                vbuf[2,t,c]=g*dz

    spread(0,ibuf0)
    for d in range(3):
        for t in range(T):
            for c in range(16): vbuf1[d,t,c]=zero
    ib=(ibuf0,ibuf0); vb=(vbuf0,vbuf1)
    def some(k,_):
        b=4*k
        for n in range(4):
            settle(jnp.maximum(b+n-1,0),vb[(n+1)%2])
            pass
            block(b+n,ib[n%2],vb[n%2])
            spread(jnp.minimum(b+n+1,CAPACITY-1),ib[(n+1)%2])
        return 0
    lax.fori_loop(0,CAPACITY//4,some,0)
    settle(CAPACITY-1,vb[1])
    for d in range(3):
        for z,ref in enumerate((fh,fe,fn,fc)):
            def red(k,_):
                for u in range(3):
                    k8=pl.multiple_of(k*24+8*u,8)
                    r=[acc[d][pl.ds((z*CAPACITY+k8)*8+q,8,stride=8),:] for q in range(8)]
                    r=((r[0]+r[1])+(r[2]+r[3]))+((r[4]+r[5])+(r[6]+r[7]))
                    if z==0: ref[d,pl.ds(k8,8),:]=ref[d,pl.ds(k8,8),:]-r
                    else: ref[d,pl.ds(k8,8),:]=-r
                return 0
            lax.fori_loop(0,CAPACITY//24,red,0)

VM = pl.BlockSpec(memory_space=pltpu.VMEM)
SM = pl.BlockSpec(memory_space=pltpu.SMEM)
HBM = pl.BlockSpec(memory_space=pltpu.HBM)
PARAMS = pltpu.CompilerParams(vmem_limit_bytes=48 * 1024 * 1024)
STAY = pltpu.CompilerParams(vmem_limit_bytes=50 * 1024 * 1024)
WIDE = pltpu.CompilerParams(vmem_limit_bytes=56 * 1024 * 1024)


def planes(count, rows=CAPACITY):
    return jax.ShapeDtypeStruct((count, rows, BLOCK), jnp.float32)


def body(positions, velocities, charges, repel_root, disperse_root, inverse_mass, move, tiles):
    inputs = (
        move.reshape(NB),
        positions.reshape(3, NB, BLOCK),
        velocities.reshape(3, NB, BLOCK),
        charges.reshape(NB, BLOCK),
        repel_root.reshape(NB, BLOCK),
        disperse_root.reshape(NB, BLOCK),
        inverse_mass.reshape(NB, BLOCK),
    )
    held = (
        [pltpu.SMEM((NB,), jnp.int32)]
        + [pltpu.VMEM((3, NB, BLOCK), jnp.float32)] * 2
        + [pltpu.VMEM((NB, BLOCK), jnp.float32)] * 4
    )
    going_up_x, going_down_x, own = pl.pallas_call(
        pack_kernel,
        out_shape=(planes(3, 24), planes(3, 24), planes(2, 24)),
        in_specs=[HBM] * 7,
        out_specs=(VM,) * 3,
        scratch_shapes=held
        + [pltpu.SMEM((18,), jnp.int32), pltpu.SemaphoreType.DMA((7,)), pltpu.VMEM((8, 24, BLOCK), jnp.float32)],
        compiler_params=WIDE,
        name="pack",
    )(*inputs)
    left = passed_along(going_up_x, 1, 0)
    right = passed_along(going_down_x, -1, 0)
    stay, staying = pl.pallas_call(
        stay_kernel,
        out_shape=(planes(10), jax.ShapeDtypeStruct((1,), jnp.int32)),
        in_specs=[HBM] * 7,
        out_specs=(VM, SM),
        scratch_shapes=held + [pltpu.SemaphoreType.DMA((7,))],
        compiler_params=STAY,
        cost_estimate=pl.CostEstimate(flops=0, bytes_accessed=6_000_000, transcendentals=0),
        name="stay",
    )(*inputs)
    up, down = pl.pallas_call(
        turn_kernel,
        out_shape=(planes(3, 24),) * 2,
        in_specs=[SM] + [VM] * 3,
        out_specs=(VM,) * 2,
        compiler_params=PARAMS,
        name="turn",
    )(staying, own, left, right)
    up = passed_along(up, 0, 1)
    down = passed_along(down, 0, -1)
    coords, rest = pl.pallas_call(
        arrive_kernel,
        out_shape=(planes(6), planes(4)),
        in_specs=[SM] + [VM] * 5,
        out_specs=(VM, VM),
        scratch_shapes=[pltpu.VMEM((10, CAPACITY + 8, BLOCK), jnp.float32)],
        compiler_params=PARAMS,
        name="arrive",
    )(staying, stay, left, right, up, down)
    east = passed_along(coords, -1, 0)
    north = passed_along(coords, 0, -1)
    corner = passed_along(north, -1, 0)
    on_home, on_east, on_north, on_corner = pl.pallas_call(
        pair_kernel,
        out_shape=(planes(3),) * 4,
        in_specs=[SM] + [VM] * 4,
        out_specs=(VM,) * 4,
        scratch_shapes=[pltpu.VMEM((6,4 * CAPACITY,128),jnp.float32)]+[pltpu.VMEM((4 * CAPACITY*8,128),jnp.float32)]*3+[pltpu.VMEM((6,16,8,128),jnp.float32)]*2+[pltpu.VMEM((3,2,16,8,128),jnp.float32)]*2+[pltpu.VMEM((17,8,128),jnp.float32)],
        compiler_params=PARAMS,
        name="pair",
    )(tiles.reshape(18, 128, 2).transpose(0, 2, 1).reshape(-1), coords, east, north, corner)
    from_corner = passed_along(on_corner, 1, 0)
    from_east = passed_along(on_east, 1, 0)
    from_north = passed_along(on_north + from_corner, 0, 1)
    out = pl.pallas_call(
        update_kernel,
        out_shape=(planes(3),) * 3,
        in_specs=[VM] * 5,
        out_specs=(VM,) * 3,
        compiler_params=PARAMS,
        name="update",
    )(on_home, from_east, from_north, coords, rest)
    return tuple(value.reshape(3, 1, 1, CAPACITY * BLOCK) for value in out)


def solution(mesh):
    vector = P(None, "gx", "gy", None)
    scalar = P("gx", "gy", None)
    return jax.shard_map(
        body,
        mesh=mesh,
        in_specs=(vector, vector) + (scalar,) * 5 + (P("gx", "gy", None, None),),
        out_specs=(vector,) * 3,
        check_vma=False,
    )
```
